256 devices in a mesh: dp: 32 (over x_hi, z, core), proto: 8 (over y, x_lo).
Axes of the slice: x: 4 (x_hi: 2, x_lo: 2; x = x_hi * 2 + x_lo), y: 4, z: 8, core: 2. Of those that a mesh axis runs over, the one named last changes fastest.
Arguments:
- view_one: bfloat16 [8192, 256], P('dp'), may hold values from -6 to 6
- view_two: bfloat16 [8192, 256], P('dp'), may hold values from -6 to 6
- prototypes: float32 [8, 16384, 256], P('proto', 'dp'), may hold values from -6 to 6
- moment_first: float32 [8, 16384, 256], P('proto', 'dp'), may hold values from -4 to 4
- moment_second: float32 [8, 16384, 256], P('proto', 'dp'), may hold values from 0.25 to 4
Outputs:
- new_prototypes: float32 [8, 16384, 256], P('proto', 'dp')
- new_first: float32 [8, 16384, 256], P('proto', 'dp')
- new_second: float32 [8, 16384, 256], P('proto', 'dp')
- proto_grad: float32 [8, 16384, 256], P('proto', 'dp')
The draws below stay inside these ranges and needn't reach their ends.
All inputs are finite; a program needn't handle non-finite values.
Results may differ from the reference program's by a relative error of at most 0.0019.
The reference program's roundings to bfloat16 on the way count: a program that leaves them out, or rounds other values in their place, can miss the bound.
Values may be sent and summed in bfloat16 or wider, within the bound.
No kernel may reach another device: no remote copies, remote signals or barrier semaphores. Data moves between devices by JAX's collectives and lax.ppermute only.
A program may use at most 128 MiB of HBM per device.

```python
import math
import jax
import jax.numpy as jnp
from jax import lax

D = 256
K = 131072
ITERS = 3
BATCH = 8192
K_DEV = 16384
N_PROTO = 8


def levels(rng, extent, shards, smallest, top_value):
    def one(dim, blocks):
        steps = jax.random.uniform(jax.random.fold_in(jax.random.fold_in(rng, 6), dim), (blocks,), jnp.float32, smallest / len(shards), top_value / len(shards))
        return jnp.repeat(jnp.exp(steps), extent[dim] // blocks).reshape((-1,) + (1,) * (len(extent) - dim - 1))

    factor_of = one(*shards[0])
    for cut in shards[1:]:
        factor_of = factor_of * one(*cut)
    return factor_of


def scatter_about(stream_key, shape, scale, reach, pieces=(), held_as=jnp.bfloat16):
    result = scale * jax.random.normal(stream_key, shape, jnp.float32)
    if pieces:
        result = result * levels(stream_key, shape, pieces, -0.22, 0.18)
    return jnp.clip(result, -reach, reach).astype(held_as)


def setup_inputs(seed: int = 0) -> dict:
    streams_of = jax.random.split(jax.random.key(seed), 6)
    return {
        "view_one": scatter_about(streams_of[0], (BATCH, D), 1.0, 6.0, ((0, 32),)),
        "view_two": scatter_about(streams_of[1], (BATCH, D), 1.0, 6.0, ((0, 32),)),
        "prototypes": scatter_about(streams_of[2], (N_PROTO, K_DEV, D), 1.0, 6.0, ((0, 8), (1, 32)), jnp.float32),
        "moment_first": scatter_about(streams_of[3], (N_PROTO, K_DEV, D), 0.5, 4.0, ((0, 8), (1, 32)), jnp.float32),
        "moment_second": jnp.clip(jnp.exp(math.log(4.0) - 2.7725887 * jax.random.uniform(streams_of[4], (N_PROTO, K_DEV, D), jnp.float32) ** levels(streams_of[4], (N_PROTO, K_DEV, D), ((0, 8), (1, 32)), -0.2, 0.2)), 0.25, 4.0),
    }


def normalize(values):
    values = values.astype(jnp.float32)
    return values / jnp.sqrt(lax.optimization_barrier(jnp.sum(values * values, axis=-1, keepdims=True)) + 1e-06)

def reference(view_one, view_two, prototypes, moment_first, moment_second):
    unit = normalize(prototypes)
    book = unit.astype(jnp.bfloat16)
    first_rows = normalize(view_one).astype(jnp.bfloat16)
    second_rows = normalize(view_two).astype(jnp.bfloat16)

    def expo(block):
        return jnp.exp(jnp.dot(first_rows, block.T, preferred_element_type=jnp.float32) / 0.05)
    expd = lax.map(expo, book)
    scale_b = jnp.ones((BATCH,), jnp.float32)
    scale_a = jnp.ones((N_PROTO, K_DEV), jnp.float32)
    for step in range(ITERS):
        columns = lax.map(lambda block: lax.optimization_barrier(jnp.sum(block * scale_b[:, None], axis=0)), expd)
        scale_a = 1.0 / (K * columns)
        row_terms = lax.map(lambda pair: lax.optimization_barrier(jnp.sum(pair[0] * pair[1][None, :], axis=1)), (expd, scale_a))
        scale_b = 1.0 / (BATCH * lax.optimization_barrier(jnp.sum(row_terms, axis=0)))

    def second_sum(block):
        scores = jnp.dot(second_rows, block.T, preferred_element_type=jnp.float32)
        return lax.optimization_barrier(jnp.sum(jnp.exp(scores / 0.1), axis=1))
    total = lax.optimization_barrier(jnp.sum(lax.map(second_sum, book), axis=0))

    def per_shard(triple):
        block, expo_block, weights = triple
        scores = jnp.dot(second_rows, block.T, preferred_element_type=jnp.float32)
        codes = BATCH * expo_block * weights[None, :] * scale_b[:, None]
        probs = jnp.exp(scores / 0.1) / total[:, None]
        grads_in = ((probs - codes) * (K / (32 * 0.1))).astype(jnp.bfloat16)
        return jnp.dot(grads_in.T, second_rows, preferred_element_type=jnp.float32)
    grads = lax.map(per_shard, (book, expd, scale_a))
    new_first = 0.9 * moment_first + 0.1 * grads
    new_second = 0.95 * moment_second + 0.05 * grads * grads
    new_prototypes = unit - 0.05 * new_first / (jnp.sqrt(new_second) + 1e-08)
    return (new_prototypes, new_first, new_second, grads)
```

```python
import jax
import jax.numpy as jnp
from jax import lax
from jax.sharding import Mesh, PartitionSpec as P

K = 131072
ITERS = 3
ROWS_BY = ("xh", "z")
COLUMN_GROUP = ("c", "y")
ROW_GROUP = ("xh", "z", "xl")


def normalize(values):
    values = values.astype(jnp.float32)
    return values / jnp.sqrt(jnp.sum(values * values, axis=-1, keepdims=True) + 1e-06)


def contract_last(left, right):
    return lax.dot_general(
        left, right, (((1,), (1,)), ((), ())), preferred_element_type=jnp.float32
    )


def share(values, axes):
    count = lax.axis_size(axes)
    return lax.all_to_all(
        jnp.broadcast_to(values[None], (count,) + values.shape), axes, 0, 0, tiled=True
    )


def body(view_one, view_two, prototypes, moment_first, moment_second):
    core, along_y = lax.axis_index("c"), lax.axis_index("y")
    unit = normalize(prototypes[0])
    book = unit.astype(jnp.bfloat16)
    local = jnp.stack(
        [normalize(view_one).astype(jnp.bfloat16), normalize(view_two).astype(jnp.bfloat16)]
    )
    rows = lax.all_gather(local, ("xh", "z", "c"), axis=1, tiled=True)
    batch_rows = rows.shape[1]

    count_y = lax.axis_size("y")
    pieces = [book] + [
        lax.ppermute(book, "y", [((i + k) % count_y, i) for i in range(count_y)])
        for k in range(1, count_y)
    ]
    mine = jnp.stack(pieces)
    other = lax.ppermute(mine, "c", [(0, 1), (1, 0)])
    both = jnp.stack([mine, other])
    group = both.shape[0] * both.shape[1]
    owned = book.shape[0]
    shelf = both.reshape(group * owned, -1)
    order = jnp.stack([(core + i) % 2 * count_y + (along_y + k) % count_y for i in range(2) for k in range(count_y)])

    part = local.shape[1] // count_y
    slices = lax.dynamic_slice_in_dim(local, along_y * part, part, 1)
    mine_one = share(slices[0], ROWS_BY).reshape(-1, local.shape[2])
    mine_two = share(slices[1], ROWS_BY).reshape(-1, local.shape[2])
    held = mine_one.shape[0]

    expd = jnp.exp(contract_last(shelf, mine_one) / 0.05)
    row_total = jnp.sum(jnp.exp(contract_last(shelf, mine_two) / 0.1), axis=0)
    scale_b = jnp.ones((held,), jnp.float32)
    for step in range(ITERS):
        columns = jnp.sum(expd * scale_b[None, :], axis=1).reshape(group, owned)
        columns = jnp.zeros_like(columns).at[order].set(columns)
        columns = jnp.sum(share(columns, COLUMN_GROUP), axis=0)
        scale_a = 1.0 / (K * columns)
        sums = jnp.sum(expd * scale_a[order].reshape(-1, 1), axis=0)
        if step == ITERS - 1:
            sums = jnp.stack([sums, row_total])
        sums = jnp.sum(share(sums, ROW_GROUP), axis=0)
        scale_b = 1.0 / (batch_rows * (sums[0] if step == ITERS - 1 else sums))
    everyone = share(jnp.stack([scale_b, sums[1]]), COLUMN_GROUP)
    everyone = everyone.reshape(2, count_y, 2, -1, part).transpose(2, 3, 0, 1, 4).reshape(2, batch_rows)
    scale_b, total = everyone
    scale_a = scale_a[order[0]]

    expd = jnp.exp(contract_last(book, rows[0]) / 0.05)
    codes = batch_rows * expd * scale_a[:, None] * scale_b[None, :]
    probs = jnp.exp(contract_last(book, rows[1]) / 0.1) / total[None, :]
    grads_in = ((probs - codes) * (K / (32 * 0.1))).astype(jnp.bfloat16)
    grad = lax.dot_general(
        grads_in, rows[1], (((1,), (0,)), ((), ())), preferred_element_type=jnp.float32
    )
    new_first = 0.9 * moment_first[0] + 0.1 * grad
    new_second = 0.95 * moment_second[0] + 0.05 * grad * grad
    new_prototypes = unit - 0.05 * new_first / (jnp.sqrt(new_second) + 1e-08)
    return (new_prototypes[None], new_first[None], new_second[None], grad[None])


def solution(mesh):
    fine = Mesh(mesh.devices.reshape(2, 8, 2, 4, 2), ("xh", "z", "c", "y", "xl"))
    dp, proto = ("xh", "z", "c"), ("y", "xl")
    owned = P(proto, dp, None)
    return jax.shard_map(
        body,
        mesh=fine,
        in_specs=(P(dp, None), P(dp, None), owned, owned, owned),
        out_specs=(owned, owned, owned, owned),
        check_vma=False,
    )
```

```python
import functools
import math

import jax
import jax.numpy as jnp
from jax import lax
from jax.experimental import pallas as pl
from jax.experimental.pallas import tpu as pltpu
from jax.sharding import Mesh, PartitionSpec as P

K = 131072
ITERS = 3
D = 256
OWNED = 512
HELD = 1024
PART = 64
GROUP = 8
BATCH = 8192
ROW_PEERS = 32
LOG2E = math.log2(math.e)
FIRST_SCALE = LOG2E / 0.05
SECOND_SCALE = LOG2E / 0.1
GRAD_SCALE = K / (32 * 0.1)
MIB = 1 << 20

VMEM = pl.BlockSpec(memory_space=pltpu.VMEM)
HBM = pl.BlockSpec(memory_space=pltpu.HBM)
ANY = pl.BlockSpec(memory_space=pl.ANY)
SMEM = pl.BlockSpec(memory_space=pltpu.SMEM)


def normalize(values):
    values = values.astype(jnp.float32)
    return values / jnp.sqrt(jnp.sum(values * values, axis=-1, keepdims=True) + 1e-06)


def contract_last(left, right):
    return lax.dot_general(
        left, right, (((1,), (1,)), ((), ())), preferred_element_type=jnp.float32
    )


def place_of(pos_ref, block):
    return (pos_ref[0] + block // 4) % 2 * 4 + (pos_ref[1] + block % 4) % 4


def book_kernel(proto_ref, book_ref):
    book_ref[...] = normalize(proto_ref[0]).astype(jnp.bfloat16)


def views_kernel(pos_ref, one_ref, two_ref, share_ref):
    for view, ref in enumerate((one_ref, two_ref)):
        rows = normalize(ref[...]).astype(jnp.bfloat16)
        for peer in range(share_ref.shape[0]):
            share_ref[peer, view] = rows


def rows_of(rows_ref, view, at, count):
    return rows_ref[at // PART : (at + count) // PART, view].reshape(count, D)


def copies_of_columns(pos_ref, columns, out_ref):
    line = lax.broadcasted_iota(jnp.int32, (GROUP, OWNED), 0)
    placed = jnp.zeros((GROUP, OWNED), jnp.float32)
    for block, values in enumerate(columns):
        placed = jnp.where(line == place_of(pos_ref, block), values, placed)
    for peer in range(GROUP):
        out_ref[peer] = placed


def expo_kernel(pos_ref, rows_ref, *refs):
    shelves, (expd_ref, out_ref) = refs[:GROUP], refs[GROUP:]
    columns = []
    for block in range(GROUP):
        shelf = shelves[block][...]
        total = jnp.zeros((8, OWNED), jnp.float32)
        for at in range(0, HELD, 256):
            tile = jnp.exp2(contract_last(rows_of(rows_ref, 0, at, 256), shelf) * FIRST_SCALE)
            expd_ref[block, at : at + 256, :] = tile
            total = total + jnp.sum(tile.reshape(32, 8, OWNED), axis=0)
        columns.append(jnp.sum(total, axis=0, keepdims=True))
    copies_of_columns(pos_ref, columns, out_ref)


def rows_as_lanes(partial_ref):
    lines = [
        jnp.sum(partial_ref[j * 128 : (j + 1) * 128, :].T, axis=0, keepdims=True) for j in range(HELD // 128)
    ]
    return jnp.concatenate(lines, axis=0)


def row_kernel(pos_ref, columns_ref, expd_ref, out_ref, scale_ref, partial_ref):
    scale_a = 1.0 / (K * jnp.sum(columns_ref[...], axis=0))
    line = lax.broadcasted_iota(jnp.int32, (GROUP, OWNED), 0)
    for block in range(GROUP):
        picked = jnp.sum(jnp.where(line == place_of(pos_ref, block), scale_a, 0.0), axis=0, keepdims=True)
        scale_ref[block] = jnp.broadcast_to(picked, (8, OWNED))

    def step(i, carry):
        at = pl.ds(pl.multiple_of(i * 64, 64), 64)
        total = jnp.zeros((8, 8, 128), jnp.float32)
        for block in range(GROUP):
            for lane in range(0, OWNED, 128):
                tile = expd_ref[block, at, lane : lane + 128].reshape(8, 8, 128)
                total = total + tile * scale_ref[block, :, lane : lane + 128][None]
        partial_ref[at, :] = total.reshape(64, 128)
        return carry

    lax.fori_loop(0, HELD // 64, step, 0)
    lines = rows_as_lanes(partial_ref)
    for peer in range(ROW_PEERS):
        out_ref[peer] = lines


def last_row_kernel(pos_ref, columns_ref, expd_ref, total_ref, out_ref, scale_ref, partial_ref):
    row_kernel(pos_ref, columns_ref, expd_ref, out_ref.at[:, 0], scale_ref, partial_ref)
    for peer in range(ROW_PEERS):
        out_ref[peer, 1] = total_ref[...]


def column_kernel(pos_ref, sums_ref, expd_ref, out_ref, scale_ref):
    scale_b = 1.0 / (BATCH * jnp.sum(sums_ref[...], axis=0))
    for j in range(HELD // 128):
        scale_ref[j * 128 : (j + 1) * 128, :] = jnp.broadcast_to(scale_b[j : j + 1, :], (128, 128)).T

    def step(i, totals):
        at = pl.ds(pl.multiple_of(i * 8, 8), 8)
        scale = scale_ref[at, :]
        return tuple(
            totals[4 * block + j] + expd_ref[block, at, 128 * j : 128 * j + 128] * scale
            for block in range(GROUP)
            for j in range(4)
        )

    zero = jnp.zeros((8, 128), jnp.float32)
    totals = lax.fori_loop(0, HELD // 8, step, (zero,) * (4 * GROUP), unroll=4)
    columns = [
        jnp.sum(jnp.concatenate(totals[4 * block : 4 * block + 4], axis=1), axis=0, keepdims=True)
        for block in range(GROUP)
    ]
    copies_of_columns(pos_ref, columns, out_ref)


def total_kernel(rows_ref, *refs):
    shelves, (out_ref, partial_ref) = refs[:GROUP], refs[GROUP:]
    partial_ref[...] = jnp.zeros_like(partial_ref)
    for block in range(GROUP):
        shelf = shelves[block][...]
        for at in range(0, HELD, 256):
            tile = jnp.exp2(contract_last(rows_of(rows_ref, 1, at, 256), shelf) * SECOND_SCALE)
            partial_ref[at : at + 256, :] += sum(tile[:, lane : lane + 128] for lane in range(0, OWNED, 128))
    out_ref[...] = rows_as_lanes(partial_ref)


def scales_kernel(sums_ref, out_ref):
    sums = jnp.sum(sums_ref[...], axis=0)
    scale_b = GRAD_SCALE / sums[0]
    scale_z = GRAD_SCALE / sums[1]
    for peer in range(out_ref.shape[0]):
        out_ref[peer, 0] = scale_b
        out_ref[peer, 1] = scale_z


def grad_kernel(half, pos_ref, scales_ref, columns_ref, book_ref, *refs):
    pieces, (out_ref, scale_ref, grads_ref) = refs[:5], refs[5:]
    scale_a = 1.0 / (K * jnp.sum(columns_ref[...], axis=0))
    line = lax.broadcasted_iota(jnp.int32, (GROUP, OWNED), 0)
    picked = jnp.sum(jnp.where(line == place_of(pos_ref, 4 * half), scale_a, 0.0), axis=0, keepdims=True)
    for j in range(OWNED // 128):
        scale_ref[j * 128 : (j + 1) * 128, :] = jnp.broadcast_to(
            picked[:, j * 128 : (j + 1) * 128], (128, 128)
        ).T
    book = book_ref[...]

    def view(block, number, at):
        if block != 2:
            return rows_of(pieces[(0, 1, None, 2)[block]], number, at, 256)
        return rows_of(pieces[3 + at // (HELD // 2)], number, at % (HELD // 2), 256)

    for block in range(4):
        place = (pos_ref[1] + block) % 4
        scale_b, scale_z = scales_ref[place, 0], scales_ref[place, 1]
        for at in range(0, HELD, 256):
            two = view(block, 1, at)
            codes = jnp.exp2(contract_last(book, view(block, 0, at)) * FIRST_SCALE)
            probs = jnp.exp2(contract_last(book, two) * SECOND_SCALE)
            tiles = []
            for j in range(0, 256, 128):
                row = (at + j) // 128
                tiles.append(
                    (
                        probs[:, j : j + 128] * scale_z[row : row + 1, :]
                        - codes[:, j : j + 128] * scale_ref[...] * scale_b[row : row + 1, :]
                    ).astype(jnp.bfloat16)
                )
            part = jnp.dot(jnp.concatenate(tiles, axis=1), two, preferred_element_type=jnp.float32)
            if block == 0 and at == 0:
                grads_ref[...] = part
            else:
                grads_ref[...] += part
    out_ref[...] = grads_ref[...]


def update_kernel(
    own_ref, other_ref, proto_ref, first_ref, second_ref, new_proto_ref, new_first_ref, new_second_ref, grad_ref
):
    grad = own_ref[...] + other_ref[...]
    new_first = 0.9 * first_ref[0] + 0.1 * grad
    new_second = 0.95 * second_ref[0] + 0.05 * grad * grad
    grad_ref[0] = grad
    new_first_ref[0] = new_first
    new_second_ref[0] = new_second
    new_proto_ref[0] = normalize(proto_ref[0]) - 0.05 * new_first / (jnp.sqrt(new_second) + 1e-08)


def params(mib):
    return pltpu.CompilerParams(vmem_limit_bytes=mib * MIB)


def f32(*shape):
    return jax.ShapeDtypeStruct(shape, jnp.float32)


def bf16(*shape):
    return jax.ShapeDtypeStruct(shape, jnp.bfloat16)


def cost(elements, size):
    return pl.CostEstimate(flops=2 * elements * D, bytes_accessed=size, transcendentals=elements)


def body(view_one, view_two, prototypes, moment_first, moment_second):
    core, along_y = lax.axis_index("c"), lax.axis_index("y")
    pos = jnp.stack([core, along_y]).astype(jnp.int32)
    groups = lax.axis_size("xh") * lax.axis_size("z")

    def exchange(copies, axes):
        return lax.all_to_all(copies, axes, 0, 0, tiled=True)

    def from_y(values, distance):
        return lax.ppermute(values, "y", [((i + distance) % 4, i) for i in range(4)])

    def from_core(values):
        return lax.ppermute(values, "c", [(0, 1), (1, 0)])

    book = pl.pallas_call(
        book_kernel,
        out_shape=bf16(OWNED, D),
        in_specs=[VMEM],
        out_specs=VMEM,
        compiler_params=params(8),
        name="book",
    )(prototypes)
    shelves = [book] + [from_y(book, k) for k in range(1, 4)]
    view_one, view_two, _ = lax.optimization_barrier((view_one, view_two, book))
    share = pl.pallas_call(
        views_kernel,
        out_shape=bf16(groups, 2, PART, D),
        grid_spec=pltpu.PrefetchScalarGridSpec(
            num_scalar_prefetch=1,
            grid=(1,),
            in_specs=[pl.BlockSpec((PART, D), lambda i, p: (p[1], 0))] * 2,
            out_specs=VMEM,
        ),
        compiler_params=params(8),
        name="views",
    )(pos, view_one, view_two)
    own_rows = exchange(share, ("xh", "z"))
    *shelves, own_rows = lax.optimization_barrier((*shelves, own_rows))
    shelves += [from_core(shelf) for shelf in shelves]

    total = pl.pallas_call(
        total_kernel,
        out_shape=f32(8, 128),
        in_specs=[VMEM] * (1 + GROUP),
        out_specs=VMEM,
        scratch_shapes=[pltpu.VMEM((HELD, 128), jnp.float32)],
        compiler_params=params(8),
        cost_estimate=cost(HELD * GROUP * OWNED, 3 * MIB),
        name="totals",
    )(own_rows, *shelves)
    *shelves, total = lax.optimization_barrier((*shelves, total))
    expd, copies = pl.pallas_call(
        expo_kernel,
        out_shape=(f32(GROUP, HELD, OWNED), f32(GROUP, GROUP, OWNED)),
        in_specs=[SMEM] + [VMEM] * (1 + GROUP),
        out_specs=(VMEM, VMEM),
        compiler_params=params(8),
        name="expo",
    )(pos, own_rows, *shelves)
    columns = exchange(copies, ("c", "y"))
    sent, columns = lax.optimization_barrier((own_rows, columns))
    after, before = from_y(sent, 1), from_y(sent, -1)
    row_scratch = [pltpu.VMEM((GROUP, 8, OWNED), jnp.float32), pltpu.VMEM((HELD, 128), jnp.float32)]
    assert ITERS == 3
    for step in range(ITERS - 1):
        copies = pl.pallas_call(
            row_kernel,
            out_shape=f32(ROW_PEERS, 8, 128),
            in_specs=[SMEM, VMEM, VMEM],
            out_specs=VMEM,
            scratch_shapes=row_scratch,
            compiler_params=params(8),
            name="row_sums",
        )(pos, columns, expd)
        sums = exchange(copies, ("xh", "z", "xl"))
        copies = pl.pallas_call(
            column_kernel,
            out_shape=f32(GROUP, GROUP, OWNED),
            in_specs=[SMEM, VMEM, VMEM],
            out_specs=VMEM,
            scratch_shapes=[pltpu.VMEM((HELD, 128), jnp.float32)],
            compiler_params=params(8),
            name="column_sums",
        )(pos, sums, expd)
        if step == 0:
            after, before, copies = lax.optimization_barrier((after, before, copies))
        else:
            far_low, far_high, copies = lax.optimization_barrier((far_low, far_high, copies))
        columns = exchange(copies, ("c", "y"))
        if step == 0:
            after, before, columns = lax.optimization_barrier((after, before, columns))
            far_low, far_high = from_y(after[: groups // 2], 1), from_y(before[groups // 2 :], -1)
    copies = pl.pallas_call(
        last_row_kernel,
        out_shape=f32(ROW_PEERS, 2, 8, 128),
        in_specs=[SMEM, VMEM, VMEM, VMEM],
        out_specs=VMEM,
        scratch_shapes=row_scratch,
        compiler_params=params(8),
        name="last_row_sums",
    )(pos, columns, expd, total)
    sums = exchange(copies, ("xh", "z", "xl"))
    copies = pl.pallas_call(
        scales_kernel,
        out_shape=f32(4, 2, 8, 128),
        in_specs=[VMEM],
        out_specs=VMEM,
        compiler_params=params(8),
        name="scales",
    )(sums)
    scales = exchange(copies, ("y",))

    def grad_of(half):
        return pl.pallas_call(
            functools.partial(grad_kernel, half),
            out_shape=f32(OWNED, D),
            in_specs=[SMEM] + [VMEM] * 8,
            out_specs=VMEM,
            scratch_shapes=[pltpu.VMEM((OWNED, 128), jnp.float32), pltpu.VMEM((OWNED, D), jnp.float32)],
            compiler_params=params(8),
            cost_estimate=cost(3 * 4 * HELD * OWNED, 6 * MIB),
            name="grad_of_own" if half == 0 else "grad_of_other",
        )(pos, scales, columns, shelves[4 * half], own_rows, after, before, far_low, far_high)

    away = grad_of(1)
    scales, away = lax.optimization_barrier((scales, away))
    own, other = grad_of(0), from_core(away)
    block = pl.BlockSpec((1, OWNED // 2, D), lambda i: (0, i, 0))
    return pl.pallas_call(
        update_kernel,
        out_shape=(f32(1, OWNED, D),) * 4,
        grid=(2,),
        in_specs=[pl.BlockSpec((OWNED // 2, D), lambda i: (i, 0))] * 2 + [block] * 3,
        out_specs=(block,) * 4,
        compiler_params=params(16),
        name="update",
    )(own, other, prototypes, moment_first, moment_second)


def solution(mesh):
    fine = Mesh(mesh.devices.reshape(2, 8, 2, 4, 2), ("xh", "z", "c", "y", "xl"))
    dp, proto = ("xh", "z", "c"), ("y", "xl")
    owned = P(proto, dp, None)
    return jax.shard_map(
        body,
        mesh=fine,
        in_specs=(P(dp, None), P(dp, None), owned, owned, owned),
        out_specs=(owned, owned, owned, owned),
        check_vma=False,
    )
```

```python
import functools
import math

import jax
import jax.numpy as jnp
from jax import lax
from jax.experimental import pallas as pl
from jax.experimental.pallas import tpu as pltpu
from jax.sharding import Mesh, PartitionSpec as P

K = 131072
ITERS = 3
D = 256
OWNED = 512
HELD = 1024
PART = 32
PLANES = 8
GROUP = 8
BATCH = 8192
ROW_PEERS = 32
LOG2E = math.log2(math.e)
FIRST_SCALE = LOG2E / 0.05
SECOND_SCALE = LOG2E / 0.1
GRAD_SCALE = K / (32 * 0.1)
MIB = 1 << 20

VMEM = pl.BlockSpec(memory_space=pltpu.VMEM)
HBM = pl.BlockSpec(memory_space=pltpu.HBM)
ANY = pl.BlockSpec(memory_space=pl.ANY)
SMEM = pl.BlockSpec(memory_space=pltpu.SMEM)


def normalize(values):
    values = values.astype(jnp.float32)
    return values / jnp.sqrt(jnp.sum(values * values, axis=-1, keepdims=True) + 1e-06)


def contract_last(left, right):
    return lax.dot_general(
        left, right, (((1,), (1,)), ((), ())), preferred_element_type=jnp.float32
    )


def place_of(pos_ref, block):
    return (pos_ref[0] + block // 4) % 2 * 4 + (pos_ref[1] + block % 4) % 4


def book_kernel(proto_ref, book_ref):
    book_ref[...] = normalize(proto_ref[0]).astype(jnp.bfloat16)


def views_kernel(pos_ref, one_ref, two_ref, share_ref):
    for view, ref in enumerate((one_ref, two_ref)):
        rows = normalize(ref[...]).astype(jnp.bfloat16)
        for peer in range(share_ref.shape[0]):
            share_ref[peer, view] = rows


def rows_of(rows_ref, view, at):
    return rows_ref[at // 256, :, view].reshape(256, D)


def copies_of_columns(pos_ref, columns, out_ref):
    line = lax.broadcasted_iota(jnp.int32, (GROUP, OWNED), 0)
    placed = jnp.zeros((GROUP, OWNED), jnp.float32)
    for block, values in enumerate(columns):
        placed = jnp.where(line == place_of(pos_ref, block), values, placed)
    for peer in range(GROUP):
        out_ref[peer] = placed


def expo_kernel(pos_ref, rows_ref, *refs):
    shelves, (expd_ref, out_ref) = refs[:GROUP], refs[GROUP:]
    columns = []
    for block in range(GROUP):
        shelf = shelves[block][...]
        total = jnp.zeros((8, OWNED), jnp.float32)
        for at in range(0, HELD, 256):
            tile = jnp.exp2(contract_last(rows_of(rows_ref, 0, at), shelf) * FIRST_SCALE)
            expd_ref[block, at : at + 256, :] = tile
            total = total + jnp.sum(tile.reshape(32, 8, OWNED), axis=0)
        columns.append(jnp.sum(total, axis=0, keepdims=True))
    copies_of_columns(pos_ref, columns, out_ref)


def rows_as_lanes(partial_ref):
    lines = [
        jnp.sum(partial_ref[j * 128 : (j + 1) * 128, :].T, axis=0, keepdims=True) for j in range(HELD // 128)
    ]
    return jnp.concatenate(lines, axis=0)


def row_kernel(pos_ref, columns_ref, expd_ref, out_ref, scale_ref, partial_ref):
    scale_a = 1.0 / (K * jnp.sum(columns_ref[...], axis=0))
    line = lax.broadcasted_iota(jnp.int32, (GROUP, OWNED), 0)
    for block in range(GROUP):
        picked = jnp.sum(jnp.where(line == place_of(pos_ref, block), scale_a, 0.0), axis=0, keepdims=True)
        scale_ref[block] = jnp.broadcast_to(picked, (8, OWNED))

    def step(i, carry):
        at = pl.ds(pl.multiple_of(i * 64, 64), 64)
        total = jnp.zeros((8, 8, 128), jnp.float32)
        for block in range(GROUP):
            for lane in range(0, OWNED, 128):
                tile = expd_ref[block, at, lane : lane + 128].reshape(8, 8, 128)
                total = total + tile * scale_ref[block, :, lane : lane + 128][None]
        partial_ref[at, :] = total.reshape(64, 128)
        return carry

    lax.fori_loop(0, HELD // 64, step, 0, unroll=16)
    lines = rows_as_lanes(partial_ref)
    for peer in range(ROW_PEERS):
        out_ref[peer] = lines


def last_row_kernel(pos_ref, columns_ref, expd_ref, total_ref, out_ref, scale_ref, partial_ref):
    row_kernel(pos_ref, columns_ref, expd_ref, out_ref.at[:, 0], scale_ref, partial_ref)
    for peer in range(ROW_PEERS):
        out_ref[peer, 1] = total_ref[...]


def column_kernel(pos_ref, sums_ref, expd_ref, out_ref, scale_ref):
    scale_b = 1.0 / (BATCH * jnp.sum(sums_ref[...], axis=0))
    for j in range(HELD // 128):
        scale_ref[j * 128 : (j + 1) * 128, :] = jnp.broadcast_to(scale_b[j : j + 1, :], (128, 128)).T

    def step(i, totals):
        at = pl.ds(pl.multiple_of(i * 8, 8), 8)
        scale = scale_ref[at, :]
        return tuple(
            totals[4 * block + j] + expd_ref[block, at, 128 * j : 128 * j + 128] * scale
            for block in range(GROUP)
            for j in range(4)
        )

    zero = jnp.zeros((8, 128), jnp.float32)
    totals = lax.fori_loop(0, HELD // 8, step, (zero,) * (4 * GROUP), unroll=16)
    columns = [
        jnp.sum(jnp.concatenate(totals[4 * block : 4 * block + 4], axis=1), axis=0, keepdims=True)
        for block in range(GROUP)
    ]
    copies_of_columns(pos_ref, columns, out_ref)


def total_kernel(rows_ref, *refs):
    shelves, (out_ref, partial_ref) = refs[:GROUP], refs[GROUP:]
    partial_ref[...] = jnp.zeros_like(partial_ref)
    for block in range(GROUP):
        shelf = shelves[block][...]
        for at in range(0, HELD, 256):
            tile = jnp.exp2(contract_last(rows_of(rows_ref, 1, at), shelf) * SECOND_SCALE)
            partial_ref[at : at + 256, :] += sum(tile[:, lane : lane + 128] for lane in range(0, OWNED, 128))
    out_ref[...] = rows_as_lanes(partial_ref)


def scales_kernel(sums_ref, out_ref):
    sums = jnp.sum(sums_ref[...], axis=0)
    scale_b = GRAD_SCALE / sums[0]
    scale_z = GRAD_SCALE / sums[1]
    for peer in range(out_ref.shape[0]):
        out_ref[peer, 0] = scale_b
        out_ref[peer, 1] = scale_z


def grad_kernel(half, pos_ref, scales_ref, columns_ref, book_ref, *refs):
    pieces, (out_ref, scale_ref, grads_ref) = refs[:5], refs[5:]
    scale_a = 1.0 / (K * jnp.sum(columns_ref[...], axis=0))
    line = lax.broadcasted_iota(jnp.int32, (GROUP, OWNED), 0)
    picked = jnp.sum(jnp.where(line == place_of(pos_ref, 4 * half), scale_a, 0.0), axis=0, keepdims=True)
    for j in range(OWNED // 128):
        scale_ref[j * 128 : (j + 1) * 128, :] = jnp.broadcast_to(
            picked[:, j * 128 : (j + 1) * 128], (128, 128)
        ).T
    book = book_ref[...]

    def view(block, number, at):
        if block != 2:
            return rows_of(pieces[(0, 1, None, 2)[block]], number, at)
        return rows_of(pieces[3 + at // (HELD // 2)], number, at % (HELD // 2))

    for block in range(4):
        place = (pos_ref[1] + block) % 4
        scale_b, scale_z = scales_ref[place, 0], scales_ref[place, 1]
        for at in range(0, HELD, 256):
            two = view(block, 1, at)
            codes = jnp.exp2(contract_last(book, view(block, 0, at)) * FIRST_SCALE)
            probs = jnp.exp2(contract_last(book, two) * SECOND_SCALE)
            tiles = []
            for j in range(0, 256, 128):
                row = (at + j) // 128
                tiles.append(
                    (
                        probs[:, j : j + 128] * scale_z[row : row + 1, :]
                        - codes[:, j : j + 128] * scale_ref[...] * scale_b[row : row + 1, :]
                    ).astype(jnp.bfloat16)
                )
            part = jnp.dot(jnp.concatenate(tiles, axis=1), two, preferred_element_type=jnp.float32)
            if block == 0 and at == 0:
                grads_ref[...] = part
            else:
                grads_ref[...] += part
    out_ref[...] = grads_ref[...]


def update_kernel(
    own_ref, other_ref, proto_ref, first_ref, second_ref, new_proto_ref, new_first_ref, new_second_ref, grad_ref
):
    grad = own_ref[...] + other_ref[...]
    new_first = 0.9 * first_ref[0] + 0.1 * grad
    new_second = 0.95 * second_ref[0] + 0.05 * grad * grad
    grad_ref[0] = grad
    new_first_ref[0] = new_first
    new_second_ref[0] = new_second
    new_proto_ref[0] = normalize(proto_ref[0]) - 0.05 * new_first / (jnp.sqrt(new_second) + 1e-08)


def params(mib):
    return pltpu.CompilerParams(vmem_limit_bytes=mib * MIB)


def f32(*shape):
    return jax.ShapeDtypeStruct(shape, jnp.float32)


def bf16(*shape):
    return jax.ShapeDtypeStruct(shape, jnp.bfloat16)


def cost(elements, size):
    return pl.CostEstimate(flops=2 * elements * D, bytes_accessed=size, transcendentals=elements)


def body(view_one, view_two, prototypes, moment_first, moment_second):
    pos = jnp.stack([lax.axis_index(name) for name in ("c", "y", "xl")]).astype(jnp.int32)

    def exchange(copies, axes):
        return lax.all_to_all(copies, axes, 0, 0, tiled=True)

    def from_y(values, distance):
        return lax.ppermute(values, "y", [((i + distance) % 4, i) for i in range(4)])

    def from_core(values):
        return lax.ppermute(values, "c", [(0, 1), (1, 0)])

    book = pl.pallas_call(
        book_kernel,
        out_shape=bf16(OWNED, D),
        in_specs=[VMEM],
        out_specs=VMEM,
        compiler_params=params(8),
        name="book",
    )(prototypes)
    share = pl.pallas_call(
        views_kernel,
        out_shape=bf16(PLANES, 2, PART, D),
        grid_spec=pltpu.PrefetchScalarGridSpec(
            num_scalar_prefetch=1,
            grid=(1,),
            in_specs=[pl.BlockSpec((PART, D), lambda i, p: (2 * p[1] + p[2], 0))] * 2,
            out_specs=VMEM,
        ),
        compiler_params=params(8),
        name="views",
    )(pos, view_one, view_two)
    shelves = [book] + [from_y(book, k) for k in range(1, 4)]
    share = exchange(share, ("z",))
    shelves[1], shelves[3], share = lax.optimization_barrier((shelves[1], shelves[3], share))
    shelves += [from_core(shelf) for shelf in shelves]
    own_rows = exchange(jnp.broadcast_to(share[None], (4,) + share.shape), ("xh", "xl"))

    total = pl.pallas_call(
        total_kernel,
        out_shape=f32(8, 128),
        in_specs=[VMEM] * (1 + GROUP),
        out_specs=VMEM,
        scratch_shapes=[pltpu.VMEM((HELD, 128), jnp.float32)],
        compiler_params=params(8),
        cost_estimate=cost(HELD * GROUP * OWNED, 3 * MIB),
        name="totals",
    )(own_rows, *shelves)
    *shelves, total = lax.optimization_barrier((*shelves, total))
    expd, copies = pl.pallas_call(
        expo_kernel,
        out_shape=(f32(GROUP, HELD, OWNED), f32(GROUP, GROUP, OWNED)),
        in_specs=[SMEM] + [VMEM] * (1 + GROUP),
        out_specs=(VMEM, VMEM),
        compiler_params=params(8),
        name="expo",
    )(pos, own_rows, *shelves)
    columns = exchange(copies, ("c", "y"))
    sent, columns = lax.optimization_barrier((own_rows, columns))
    after, before = from_y(sent, 1), from_y(sent, -1)
    row_scratch = [pltpu.VMEM((GROUP, 8, OWNED), jnp.float32), pltpu.VMEM((HELD, 128), jnp.float32)]
    assert ITERS == 3
    for step in range(ITERS - 1):
        copies = pl.pallas_call(
            row_kernel,
            out_shape=f32(ROW_PEERS, 8, 128),
            in_specs=[SMEM, VMEM, VMEM],
            out_specs=VMEM,
            scratch_shapes=row_scratch,
            compiler_params=params(8),
            name="row_sums",
        )(pos, columns, expd)
        sums = exchange(copies, ("xh", "z", "xl"))
        copies = pl.pallas_call(
            column_kernel,
            out_shape=f32(GROUP, GROUP, OWNED),
            in_specs=[SMEM, VMEM, VMEM],
            out_specs=VMEM,
            scratch_shapes=[pltpu.VMEM((HELD, 128), jnp.float32)],
            compiler_params=params(8),
            name="column_sums",
        )(pos, sums, expd)
        if step == 0:
            after, before, copies = lax.optimization_barrier((after, before, copies))
        else:
            far_low, far_high, copies = lax.optimization_barrier((far_low, far_high, copies))
        columns = exchange(copies, ("c", "y"))
        if step == 0:
            after, before, columns = lax.optimization_barrier((after, before, columns))
            far_low, far_high = from_y(after[:2], 1), from_y(before[2:], -1)
    copies = pl.pallas_call(
        last_row_kernel,
        out_shape=f32(ROW_PEERS, 2, 8, 128),
        in_specs=[SMEM, VMEM, VMEM, VMEM],
        out_specs=VMEM,
        scratch_shapes=row_scratch,
        compiler_params=params(8),
        name="last_row_sums",
    )(pos, columns, expd, total)
    sums = exchange(copies, ("xh", "z", "xl"))
    copies = pl.pallas_call(
        scales_kernel,
        out_shape=f32(4, 2, 8, 128),
        in_specs=[VMEM],
        out_specs=VMEM,
        compiler_params=params(8),
        name="scales",
    )(sums)
    scales = exchange(copies, ("y",))

    def grad_of(half):
        return pl.pallas_call(
            functools.partial(grad_kernel, half),
            out_shape=f32(OWNED, D),
            in_specs=[SMEM] + [VMEM] * 8,
            out_specs=VMEM,
            scratch_shapes=[pltpu.VMEM((OWNED, 128), jnp.float32), pltpu.VMEM((OWNED, D), jnp.float32)],
            compiler_params=params(8),
            cost_estimate=cost(3 * 4 * HELD * OWNED, 6 * MIB),
            name="grad_of_own" if half == 0 else "grad_of_other",
        )(pos, scales, columns, shelves[4 * half], own_rows, after, before, far_low, far_high)

    away = grad_of(1)
    scales, away = lax.optimization_barrier((scales, away))
    own, other = grad_of(0), from_core(away)
    block = pl.BlockSpec((1, OWNED // 2, D), lambda i: (0, i, 0))
    return pl.pallas_call(
        update_kernel,
        out_shape=(f32(1, OWNED, D),) * 4,
        grid=(2,),
        in_specs=[pl.BlockSpec((OWNED // 2, D), lambda i: (i, 0))] * 2 + [block] * 3,
        out_specs=(block,) * 4,
        compiler_params=params(16),
        name="update",
    )(own, other, prototypes, moment_first, moment_second)


def solution(mesh):
    fine = Mesh(mesh.devices.reshape(2, 8, 2, 4, 2), ("xh", "z", "c", "y", "xl"))
    dp, proto = ("xh", "z", "c"), ("y", "xl")
    owned = P(proto, dp, None)
    return jax.shard_map(
        body,
        mesh=fine,
        in_specs=(P(dp, None), P(dp, None), owned, owned, owned),
        out_specs=(owned, owned, owned, owned),
        check_vma=False,
    )
```

```python
import functools
import math

import jax
import jax.numpy as jnp
from jax import lax
from jax.experimental import pallas as pl
from jax.experimental.pallas import tpu as pltpu
from jax.sharding import Mesh, PartitionSpec as P

K = 131072
ITERS = 3
D = 256
OWNED = 512
HELD = 1024
PART = 32
PLANES = 8
GROUP = 8
BATCH = 8192
ROW_PEERS = 32
LOG2E = math.log2(math.e)
FIRST_SCALE = LOG2E / 0.05
SECOND_SCALE = LOG2E / 0.1
GRAD_SCALE = K / (32 * 0.1)
MIB = 1 << 20

VMEM = pl.BlockSpec(memory_space=pltpu.VMEM)
HBM = pl.BlockSpec(memory_space=pltpu.HBM)
ANY = pl.BlockSpec(memory_space=pl.ANY)
SMEM = pl.BlockSpec(memory_space=pltpu.SMEM)


def normalize(values):
    values = values.astype(jnp.float32)
    return values / jnp.sqrt(jnp.sum(values * values, axis=-1, keepdims=True) + 1e-06)


def contract_last(left, right):
    return lax.dot_general(
        left, right, (((1,), (1,)), ((), ())), preferred_element_type=jnp.float32
    )


def place_of(pos_ref, block):
    return (pos_ref[0] + block // 4) % 2 * 4 + (pos_ref[1] + block % 4) % 4


def book_kernel(proto_ref, book_ref):
    book_ref[...] = normalize(proto_ref[0]).astype(jnp.bfloat16)


def views_kernel(views_ref, share_ref):
    for view in range(2):
        rows = normalize(views_ref[view]).astype(jnp.bfloat16)
        for peer in range(share_ref.shape[0]):
            share_ref[peer, view] = rows


def rows_of(rows_ref, view, at):
    return rows_ref[at // 256, :, view].reshape(256, D)


def copies_of_columns(pos_ref, columns, out_ref):
    line = lax.broadcasted_iota(jnp.int32, (GROUP, OWNED), 0)
    placed = jnp.zeros((GROUP, OWNED), jnp.float32)
    for block, values in enumerate(columns):
        placed = jnp.where(line == place_of(pos_ref, block), values, placed)
    for peer in range(GROUP):
        out_ref[peer] = placed


def expo_kernel(pos_ref, rows_ref, *refs):
    shelves, (expd_ref, out_ref) = refs[:GROUP], refs[GROUP:]
    columns = []
    for block in range(GROUP):
        shelf = shelves[block][...]
        total = jnp.zeros((8, OWNED), jnp.float32)
        for at in range(0, HELD, 256):
            tile = jnp.exp2(contract_last(rows_of(rows_ref, 0, at), shelf) * FIRST_SCALE)
            expd_ref[block, at : at + 256, :] = tile
            total = total + jnp.sum(tile.reshape(32, 8, OWNED), axis=0)
        columns.append(jnp.sum(total, axis=0, keepdims=True))
    copies_of_columns(pos_ref, columns, out_ref)


def rows_as_lanes(partial_ref):
    lines = [
        jnp.sum(partial_ref[j * 128 : (j + 1) * 128, :].T, axis=0, keepdims=True) for j in range(HELD // 128)
    ]
    return jnp.concatenate(lines, axis=0)


def row_kernel(pos_ref, columns_ref, expd_ref, out_ref, scale_ref, partial_ref):
    scale_a = 1.0 / (K * jnp.sum(columns_ref[...], axis=0))
    line = lax.broadcasted_iota(jnp.int32, (GROUP, OWNED), 0)
    for block in range(GROUP):
        picked = jnp.sum(jnp.where(line == place_of(pos_ref, block), scale_a, 0.0), axis=0, keepdims=True)
        scale_ref[block] = jnp.broadcast_to(picked, (8, OWNED))

    def step(i, carry):
        at = pl.ds(pl.multiple_of(i * 64, 64), 64)
        total = jnp.zeros((8, 8, 128), jnp.float32)
        for block in range(GROUP):
            for lane in range(0, OWNED, 128):
                tile = expd_ref[block, at, lane : lane + 128].reshape(8, 8, 128)
                total = total + tile * scale_ref[block, :, lane : lane + 128][None]
        partial_ref[at, :] = total.reshape(64, 128)
        return carry

    lax.fori_loop(0, HELD // 64, step, 0, unroll=16)
    lines = rows_as_lanes(partial_ref)
    for peer in range(ROW_PEERS):
        out_ref[peer] = lines


def last_row_kernel(pos_ref, columns_ref, expd_ref, total_ref, out_ref, scale_ref, partial_ref):
    row_kernel(pos_ref, columns_ref, expd_ref, out_ref.at[:, 0], scale_ref, partial_ref)
    for peer in range(ROW_PEERS):
        out_ref[peer, 1] = total_ref[...]


def column_kernel(pos_ref, sums_ref, expd_ref, out_ref, scale_ref):
    scale_b = 1.0 / (BATCH * jnp.sum(sums_ref[...], axis=0))
    for j in range(HELD // 128):
        scale_ref[j * 128 : (j + 1) * 128, :] = jnp.broadcast_to(scale_b[j : j + 1, :], (128, 128)).T

    def step(i, totals):
        at = pl.ds(pl.multiple_of(i * 8, 8), 8)
        scale = scale_ref[at, :]
        return tuple(
            totals[4 * block + j] + expd_ref[block, at, 128 * j : 128 * j + 128] * scale
            for block in range(GROUP)
            for j in range(4)
        )

    zero = jnp.zeros((8, 128), jnp.float32)
    totals = lax.fori_loop(0, HELD // 8, step, (zero,) * (4 * GROUP), unroll=16)
    columns = [
        jnp.sum(jnp.concatenate(totals[4 * block : 4 * block + 4], axis=1), axis=0, keepdims=True)
        for block in range(GROUP)
    ]
    copies_of_columns(pos_ref, columns, out_ref)


def total_kernel(rows_ref, *refs):
    shelves, (out_ref, partial_ref) = refs[:GROUP], refs[GROUP:]
    partial_ref[...] = jnp.zeros_like(partial_ref)
    for block in range(GROUP):
        shelf = shelves[block][...]
        for at in range(0, HELD, 256):
            tile = jnp.exp2(contract_last(rows_of(rows_ref, 1, at), shelf) * SECOND_SCALE)
            partial_ref[at : at + 256, :] += sum(tile[:, lane : lane + 128] for lane in range(0, OWNED, 128))
    out_ref[...] = rows_as_lanes(partial_ref)


def scales_kernel(sums_ref, out_ref):
    out_ref[...] = GRAD_SCALE / jnp.sum(sums_ref[...], axis=0)


def grad_kernel(halves, blocks, pos_ref, columns_ref, *refs):
    count = len(halves)
    refs = list(refs)
    books = [refs.pop(0) for _ in halves]
    scales = [refs.pop(0) for _ in blocks]
    rows = [[refs.pop(0) for _ in range(2 if block == 2 else 1)] for block in blocks]
    before = [refs.pop(0) for _ in halves] if 0 not in blocks else None
    outs, scale_ref = refs[:count], refs[count]
    scale_a = 1.0 / (K * jnp.sum(columns_ref[...], axis=0))
    line = lax.broadcasted_iota(jnp.int32, (GROUP, OWNED), 0)
    for i, half in enumerate(halves):
        picked = jnp.sum(jnp.where(line == place_of(pos_ref, 4 * half), scale_a, 0.0), axis=0, keepdims=True)
        for j in range(OWNED // 128):
            scale_ref[j * 128 : (j + 1) * 128, :] = jnp.broadcast_to(
                picked[:, j * 128 : (j + 1) * 128], (128, 128)
            ).T
        book = books[i][...]
        fresh = before is None
        for pieces, scale in zip(rows, scales):
            scale_b, scale_z = scale[0], scale[1]
            size = HELD // len(pieces)
            for at in range(0, HELD, 256):
                piece = pieces[at // size]
                two = rows_of(piece, 1, at % size)
                codes = jnp.exp2(contract_last(book, rows_of(piece, 0, at % size)) * FIRST_SCALE)
                probs = jnp.exp2(contract_last(book, two) * SECOND_SCALE)
                tiles = []
                for j in range(0, 256, 128):
                    row = (at + j) // 128
                    tiles.append(
                        (
                            probs[:, j : j + 128] * scale_z[row : row + 1, :]
                            - codes[:, j : j + 128] * scale_ref[...] * scale_b[row : row + 1, :]
                        ).astype(jnp.bfloat16)
                    )
                part = jnp.dot(jnp.concatenate(tiles, axis=1), two, preferred_element_type=jnp.float32)
                if fresh:
                    outs[i][...] = part
                elif before is not None and at == 0 and pieces is rows[0]:
                    outs[i][...] = before[i][...] + part
                else:
                    outs[i][...] += part
                fresh = False


def update_kernel(
    own_ref, other_ref, proto_ref, first_ref, second_ref, new_proto_ref, new_first_ref, new_second_ref, grad_ref
):
    grad = own_ref[...] + other_ref[...]
    new_first = 0.9 * first_ref[0] + 0.1 * grad
    new_second = 0.95 * second_ref[0] + 0.05 * grad * grad
    grad_ref[0] = grad
    new_first_ref[0] = new_first
    new_second_ref[0] = new_second
    new_proto_ref[0] = normalize(proto_ref[0]) - 0.05 * new_first / (jnp.sqrt(new_second) + 1e-08)


def params(mib):
    return pltpu.CompilerParams(vmem_limit_bytes=mib * MIB)


def f32(*shape):
    return jax.ShapeDtypeStruct(shape, jnp.float32)


def bf16(*shape):
    return jax.ShapeDtypeStruct(shape, jnp.bfloat16)


def cost(elements, size):
    return pl.CostEstimate(flops=2 * elements * D, bytes_accessed=size, transcendentals=elements)


def body(view_one, view_two, prototypes, moment_first, moment_second):
    pos = jnp.stack([lax.axis_index(name) for name in ("c", "y", "xl")]).astype(jnp.int32)

    def exchange(copies, axes):
        return lax.all_to_all(copies, axes, 0, 0, tiled=True)

    def from_y(values, distance):
        return lax.ppermute(values, "y", [((i + distance) % 4, i) for i in range(4)])

    def from_core(values):
        return lax.ppermute(values, "c", [(0, 1), (1, 0)])

    book = pl.pallas_call(
        book_kernel,
        out_shape=bf16(OWNED, D),
        in_specs=[VMEM],
        out_specs=VMEM,
        compiler_params=params(8),
        name="book",
    )(prototypes)
    start = (2 * pos[1] + pos[2]) * PART
    parts = jnp.stack([lax.dynamic_slice_in_dim(view, start, PART) for view in (view_one, view_two)])
    share = pl.pallas_call(
        views_kernel,
        out_shape=bf16(PLANES, 2, PART, D),
        in_specs=[VMEM],
        out_specs=VMEM,
        compiler_params=params(8),
        name="views",
    )(parts)
    shelves = [book] + [from_y(book, k) for k in range(1, 4)]
    share = exchange(share, ("z",))
    shelves[1], shelves[3], share = lax.optimization_barrier((shelves[1], shelves[3], share))
    shelves += [from_core(shelf) for shelf in shelves]
    own_rows = exchange(jnp.broadcast_to(share[None], (4,) + share.shape), ("xh", "xl"))

    expd, copies = pl.pallas_call(
        expo_kernel,
        out_shape=(f32(GROUP, HELD, OWNED), f32(GROUP, GROUP, OWNED)),
        in_specs=[SMEM] + [VMEM] * (1 + GROUP),
        out_specs=(VMEM, VMEM),
        compiler_params=params(8),
        name="expo",
    )(pos, own_rows, *shelves)
    columns = exchange(copies, ("c", "y"))
    sent, columns = lax.optimization_barrier((own_rows, columns))
    after, before = from_y(sent, 1), from_y(sent, -1)
    total = pl.pallas_call(
        total_kernel,
        out_shape=f32(8, 128),
        in_specs=[VMEM] * (1 + GROUP),
        out_specs=VMEM,
        scratch_shapes=[pltpu.VMEM((HELD, 128), jnp.float32)],
        compiler_params=params(8),
        cost_estimate=cost(HELD * GROUP * OWNED, 3 * MIB),
        name="totals",
    )(sent, *shelves)
    columns, total = lax.optimization_barrier((columns, total))
    row_scratch = [pltpu.VMEM((GROUP, 8, OWNED), jnp.float32), pltpu.VMEM((HELD, 128), jnp.float32)]
    assert ITERS == 3
    for step in range(ITERS - 1):
        copies = pl.pallas_call(
            row_kernel,
            out_shape=f32(ROW_PEERS, 8, 128),
            in_specs=[SMEM, VMEM, VMEM],
            out_specs=VMEM,
            scratch_shapes=row_scratch,
            compiler_params=params(8),
            name="row_sums",
        )(pos, columns, expd)
        if step == 1:
            high, copies = lax.optimization_barrier((high, copies))
            far_high = from_y(high, -1)
        sums = exchange(copies, ("xh", "z", "xl"))
        copies = pl.pallas_call(
            column_kernel,
            out_shape=f32(GROUP, GROUP, OWNED),
            in_specs=[SMEM, VMEM, VMEM],
            out_specs=VMEM,
            scratch_shapes=[pltpu.VMEM((HELD, 128), jnp.float32)],
            compiler_params=params(8),
            name="column_sums",
        )(pos, sums, expd)
        if step == 0:
            after, before, copies = lax.optimization_barrier((after, before, copies))
        else:
            far_low, far_high, copies = lax.optimization_barrier((far_low, far_high, copies))
        columns = exchange(copies, ("c", "y"))
        if step == 0:
            after, before, columns = lax.optimization_barrier((after, before, columns))
            low, high = after[:2], before[2:]
            far_low = from_y(low, 1)
    copies = pl.pallas_call(
        last_row_kernel,
        out_shape=f32(ROW_PEERS, 2, 8, 128),
        in_specs=[SMEM, VMEM, VMEM, VMEM],
        out_specs=VMEM,
        scratch_shapes=row_scratch,
        compiler_params=params(8),
        name="last_row_sums",
    )(pos, columns, expd, total)
    sums = exchange(copies, ("xh", "z", "xl"))
    copies = pl.pallas_call(
        scales_kernel,
        out_shape=f32(2, 8, 128),
        in_specs=[VMEM],
        out_specs=VMEM,
        compiler_params=params(8),
        name="scales",
    )(sums)
    scales = [copies] + [from_y(copies, k) for k in range(1, 4)]
    row_blocks = [[own_rows], [after], [far_low, far_high], [before]]

    def grad_of(halves, blocks, sums_so_far, name):
        operands = [shelves[4 * half] for half in halves] + [scales[block] for block in blocks]
        operands += [piece for block in blocks for piece in row_blocks[block]] + sums_so_far
        return pl.pallas_call(
            functools.partial(grad_kernel, halves, blocks),
            out_shape=[f32(OWNED, D)] * len(halves),
            in_specs=[SMEM] + [VMEM] * (1 + len(operands)),
            out_specs=[VMEM] * len(halves),
            scratch_shapes=[pltpu.VMEM((OWNED, 128), jnp.float32)],
            compiler_params=params(8),
            cost_estimate=cost(3 * len(halves) * len(blocks) * HELD * OWNED, 6 * MIB),
            name=name,
        )(pos, columns, *operands)

    own, away = grad_of((0, 1), (0,), [], "grad_of_own_rows")
    (away,) = grad_of((1,), (1, 3, 2), [away], "grad_of_other")
    own, away = lax.optimization_barrier((own, away))
    other = from_core(away)
    (own,) = grad_of((0,), (1, 3, 2), [own], "grad_of_own")
    block = pl.BlockSpec((1, OWNED // 2, D), lambda i: (0, i, 0))
    return pl.pallas_call(
        update_kernel,
        out_shape=(f32(1, OWNED, D),) * 4,
        grid=(2,),
        in_specs=[pl.BlockSpec((OWNED // 2, D), lambda i: (i, 0))] * 2 + [block] * 3,
        out_specs=(block,) * 4,
        compiler_params=params(16),
        name="update",
    )(own, other, prototypes, moment_first, moment_second)


def solution(mesh):
    fine = Mesh(mesh.devices.reshape(2, 8, 2, 4, 2), ("xh", "z", "c", "y", "xl"))
    dp, proto = ("xh", "z", "c"), ("y", "xl")
    owned = P(proto, dp, None)
    return jax.shard_map(
        body,
        mesh=fine,
        in_specs=(P(dp, None), P(dp, None), owned, owned, owned),
        out_specs=(owned, owned, owned, owned),
        check_vma=False,
    )
```

```python
import functools
import math

import jax
import jax.numpy as jnp
from jax import lax
from jax.experimental import pallas as pl
from jax.experimental.pallas import tpu as pltpu
from jax.sharding import Mesh, PartitionSpec as P

K = 131072
ITERS = 3
D = 256
OWNED = 512
HELD = 1024
PART = 32
PLANES = 8
GROUP = 8
BATCH = 8192
ROW_PEERS = 32
LOG2E = math.log2(math.e)
FIRST_SCALE = LOG2E / 0.05
SECOND_SCALE = LOG2E / 0.1
GRAD_SCALE = K / (32 * 0.1)
MIB = 1 << 20

VMEM = pl.BlockSpec(memory_space=pltpu.VMEM)
HBM = pl.BlockSpec(memory_space=pltpu.HBM)
ANY = pl.BlockSpec(memory_space=pl.ANY)
SMEM = pl.BlockSpec(memory_space=pltpu.SMEM)


def normalize(values):
    values = values.astype(jnp.float32)
    return values / jnp.sqrt(jnp.sum(values * values, axis=-1, keepdims=True) + 1e-06)


def contract_last(left, right):
    return lax.dot_general(
        left, right, (((1,), (1,)), ((), ())), preferred_element_type=jnp.float32
    )


def place_of(pos_ref, block):
    return (pos_ref[0] + block // 4) % 2 * 4 + (pos_ref[1] + block % 4) % 4


def book_kernel(proto_ref, book_ref):
    book_ref[...] = normalize(proto_ref[0]).astype(jnp.bfloat16)


def views_kernel(views_ref, share_ref):
    for view in range(2):
        rows = normalize(views_ref[view]).astype(jnp.bfloat16)
        for peer in range(share_ref.shape[0]):
            share_ref[peer, view] = rows


def rows_of(rows_ref, view, at):
    return rows_ref[at // 256, :, view].reshape(256, D)


def copies_of_columns(pos_ref, columns, out_ref):
    line = lax.broadcasted_iota(jnp.int32, (GROUP, OWNED), 0)
    placed = jnp.zeros((GROUP, OWNED), jnp.float32)
    for block, values in enumerate(columns):
        placed = jnp.where(line == place_of(pos_ref, block), values, placed)
    for peer in range(GROUP):
        out_ref[peer] = placed


def expo_kernel(pos_ref, rows_ref, *refs):
    shelves, (expd_ref, out_ref) = refs[:GROUP], refs[GROUP:]
    columns = []
    for block in range(GROUP):
        shelf = shelves[block][...]
        total = jnp.zeros((8, OWNED), jnp.float32)
        for at in range(0, HELD, 256):
            tile = jnp.exp2(contract_last(rows_of(rows_ref, 0, at), shelf) * FIRST_SCALE)
            expd_ref[block, at : at + 256, :] = tile
            total = total + jnp.sum(tile.reshape(32, 8, OWNED), axis=0)
        columns.append(jnp.sum(total, axis=0, keepdims=True))
    copies_of_columns(pos_ref, columns, out_ref)


def rows_as_lanes(partial_ref):
    lines = [
        jnp.sum(partial_ref[j * 128 : (j + 1) * 128, :].T, axis=0, keepdims=True) for j in range(HELD // 128)
    ]
    return jnp.concatenate(lines, axis=0)


def row_kernel(pos_ref, columns_ref, expd_ref, out_ref, scale_ref, partial_ref):
    scale_a = 1.0 / (K * jnp.sum(columns_ref[...], axis=0))
    line = lax.broadcasted_iota(jnp.int32, (GROUP, OWNED), 0)
    for block in range(GROUP):
        picked = jnp.sum(jnp.where(line == place_of(pos_ref, block), scale_a, 0.0), axis=0, keepdims=True)
        scale_ref[block] = jnp.broadcast_to(picked, (8, OWNED))

    def step(i, carry):
        at = pl.ds(pl.multiple_of(i * 64, 64), 64)
        total = jnp.zeros((8, 8, 128), jnp.float32)
        for block in range(GROUP):
            for lane in range(0, OWNED, 128):
                tile = expd_ref[block, at, lane : lane + 128].reshape(8, 8, 128)
                total = total + tile * scale_ref[block, :, lane : lane + 128][None]
        partial_ref[at, :] = total.reshape(64, 128)
        return carry

    lax.fori_loop(0, HELD // 64, step, 0, unroll=16)
    lines = rows_as_lanes(partial_ref)
    for peer in range(ROW_PEERS):
        out_ref[peer] = lines


def last_row_kernel(pos_ref, columns_ref, expd_ref, total_ref, out_ref, scale_ref, partial_ref):
    row_kernel(pos_ref, columns_ref, expd_ref, out_ref.at[:, 0], scale_ref, partial_ref)
    for peer in range(ROW_PEERS):
        out_ref[peer, 1] = total_ref[...]


def column_kernel(pos_ref, sums_ref, expd_ref, out_ref, scale_ref):
    scale_b = 1.0 / (BATCH * jnp.sum(sums_ref[...], axis=0))
    for j in range(HELD // 128):
        scale_ref[j * 128 : (j + 1) * 128, :] = jnp.broadcast_to(scale_b[j : j + 1, :], (128, 128)).T

    def step(i, totals):
        at = pl.ds(pl.multiple_of(i * 8, 8), 8)
        scale = scale_ref[at, :]
        return tuple(
            totals[4 * block + j] + expd_ref[block, at, 128 * j : 128 * j + 128] * scale
            for block in range(GROUP)
            for j in range(4)
        )

    zero = jnp.zeros((8, 128), jnp.float32)
    totals = lax.fori_loop(0, HELD // 8, step, (zero,) * (4 * GROUP), unroll=16)
    columns = [
        jnp.sum(jnp.concatenate(totals[4 * block : 4 * block + 4], axis=1), axis=0, keepdims=True)
        for block in range(GROUP)
    ]
    copies_of_columns(pos_ref, columns, out_ref)


def total_kernel(rows_ref, *refs):
    shelves, (out_ref, partial_ref) = refs[:GROUP], refs[GROUP:]
    partial_ref[...] = jnp.zeros_like(partial_ref)
    for block in range(GROUP):
        shelf = shelves[block][...]
        for at in range(0, HELD, 256):
            tile = jnp.exp2(contract_last(rows_of(rows_ref, 1, at), shelf) * SECOND_SCALE)
            partial_ref[at : at + 256, :] += sum(tile[:, lane : lane + 128] for lane in range(0, OWNED, 128))
    out_ref[...] = rows_as_lanes(partial_ref)


def scales_kernel(sums_ref, out_ref):
    out_ref[...] = GRAD_SCALE / jnp.sum(sums_ref[...], axis=0)


def grad_kernel(halves, blocks, pos_ref, columns_ref, *refs):
    count = len(halves)
    refs = list(refs)
    books = [refs.pop(0) for _ in halves]
    scales = [refs.pop(0) for _ in blocks]
    rows = [[refs.pop(0) for _ in range(2 if block == 2 else 1)] for block in blocks]
    before = [refs.pop(0) for _ in halves] if 0 not in blocks else None
    outs, scale_ref = refs[:count], refs[count]
    scale_a = 1.0 / (K * jnp.sum(columns_ref[...], axis=0))
    line = lax.broadcasted_iota(jnp.int32, (GROUP, OWNED), 0)
    for i, half in enumerate(halves):
        picked = jnp.sum(jnp.where(line == place_of(pos_ref, 4 * half), scale_a, 0.0), axis=0, keepdims=True)
        for j in range(OWNED // 128):
            scale_ref[j * 128 : (j + 1) * 128, :] = jnp.broadcast_to(
                picked[:, j * 128 : (j + 1) * 128], (128, 128)
            ).T
        book = books[i][...]
        fresh = before is None
        for pieces, scale in zip(rows, scales):
            scale_b, scale_z = scale[0], scale[1]
            size = HELD // len(pieces)
            for at in range(0, HELD, 256):
                piece = pieces[at // size]
                two = rows_of(piece, 1, at % size)
                codes = jnp.exp2(contract_last(book, rows_of(piece, 0, at % size)) * FIRST_SCALE)
                probs = jnp.exp2(contract_last(book, two) * SECOND_SCALE)
                tiles = []
                for j in range(0, 256, 128):
                    row = (at + j) // 128
                    tiles.append(
                        (
                            probs[:, j : j + 128] * scale_z[row : row + 1, :]
                            - codes[:, j : j + 128] * scale_ref[...] * scale_b[row : row + 1, :]
                        ).astype(jnp.bfloat16)
                    )
                part = jnp.dot(jnp.concatenate(tiles, axis=1), two, preferred_element_type=jnp.float32)
                if fresh:
                    outs[i][...] = part
                elif before is not None and at == 0 and pieces is rows[0]:
                    outs[i][...] = before[i][...] + part
                else:
                    outs[i][...] += part
                fresh = False


def update_kernel(
    own_ref, other_ref, proto_ref, first_ref, second_ref, new_proto_ref, new_first_ref, new_second_ref, grad_ref
):
    grad = own_ref[...] + other_ref[...]
    new_first = 0.9 * first_ref[0] + 0.1 * grad
    new_second = 0.95 * second_ref[0] + 0.05 * grad * grad
    grad_ref[0] = grad
    new_first_ref[0] = new_first
    new_second_ref[0] = new_second
    new_proto_ref[0] = normalize(proto_ref[0]) - 0.05 * new_first / (jnp.sqrt(new_second) + 1e-08)


def params(mib):
    return pltpu.CompilerParams(vmem_limit_bytes=mib * MIB)


def f32(*shape):
    return jax.ShapeDtypeStruct(shape, jnp.float32)


def bf16(*shape):
    return jax.ShapeDtypeStruct(shape, jnp.bfloat16)


def cost(elements, size):
    return pl.CostEstimate(flops=2 * elements * D, bytes_accessed=size, transcendentals=elements)


def body(view_one, view_two, prototypes, moment_first, moment_second):
    pos = jnp.stack([lax.axis_index(name) for name in ("c", "y", "xl")]).astype(jnp.int32)

    def exchange(copies, axes):
        return lax.all_to_all(copies, axes, 0, 0, tiled=True)

    def from_y(values, distance):
        return lax.ppermute(values, "y", [((i + distance) % 4, i) for i in range(4)])

    def from_core(values):
        return lax.ppermute(values, "c", [(0, 1), (1, 0)])

    book = pl.pallas_call(
        book_kernel,
        out_shape=bf16(OWNED, D),
        in_specs=[VMEM],
        out_specs=VMEM,
        compiler_params=params(8),
        name="book",
    )(prototypes)
    start = (2 * pos[1] + pos[2]) * PART
    parts = jnp.stack([lax.dynamic_slice_in_dim(view, start, PART) for view in (view_one, view_two)])
    share = pl.pallas_call(
        views_kernel,
        out_shape=bf16(PLANES, 2, PART, D),
        in_specs=[VMEM],
        out_specs=VMEM,
        compiler_params=params(8),
        name="views",
    )(parts)
    shelves = [book] + [from_y(book, k) for k in range(1, 4)]
    share = exchange(share, ("z",))
    shelves[1], shelves[3], share = lax.optimization_barrier((shelves[1], shelves[3], share))
    shelves += [from_core(shelf) for shelf in shelves]
    own_rows = exchange(jnp.broadcast_to(share[None], (4,) + share.shape), ("xh", "xl"))

    expd, copies = pl.pallas_call(
        expo_kernel,
        out_shape=(f32(GROUP, HELD, OWNED), f32(GROUP, GROUP, OWNED)),
        in_specs=[SMEM] + [VMEM] * (1 + GROUP),
        out_specs=(VMEM, VMEM),
        compiler_params=params(8),
        name="expo",
    )(pos, own_rows, *shelves)
    columns = exchange(copies, ("c", "y"))
    sent, columns = lax.optimization_barrier((own_rows, columns))
    after, before = from_y(sent, 1), from_y(sent, -1)
    total = pl.pallas_call(
        total_kernel,
        out_shape=f32(8, 128),
        in_specs=[VMEM] * (1 + GROUP),
        out_specs=VMEM,
        scratch_shapes=[pltpu.VMEM((HELD, 128), jnp.float32)],
        compiler_params=params(8),
        cost_estimate=cost(HELD * GROUP * OWNED, 3 * MIB),
        name="totals",
    )(sent, *shelves)
    columns, total = lax.optimization_barrier((columns, total))
    row_scratch = [pltpu.VMEM((GROUP, 8, OWNED), jnp.float32), pltpu.VMEM((HELD, 128), jnp.float32)]
    assert ITERS == 3
    for step in range(ITERS - 1):
        copies = pl.pallas_call(
            row_kernel,
            out_shape=f32(ROW_PEERS, 8, 128),
            in_specs=[SMEM, VMEM, VMEM],
            out_specs=VMEM,
            scratch_shapes=row_scratch,
            compiler_params=params(8),
            name="row_sums",
        )(pos, columns, expd)
        if step == 1:
            high, copies = lax.optimization_barrier((high, copies))
            far_high = from_y(high, -1)
        sums = exchange(copies, ("z", "xh", "xl"))
        copies = pl.pallas_call(
            column_kernel,
            out_shape=f32(GROUP, GROUP, OWNED),
            in_specs=[SMEM, VMEM, VMEM],
            out_specs=VMEM,
            scratch_shapes=[pltpu.VMEM((HELD, 128), jnp.float32)],
            compiler_params=params(8),
            name="column_sums",
        )(pos, sums, expd)
        if step == 0:
            after, before, copies = lax.optimization_barrier((after, before, copies))
        else:
            far_low, far_high, copies = lax.optimization_barrier((far_low, far_high, copies))
        columns = exchange(copies, ("c", "y"))
        if step == 0:
            after, before, columns = lax.optimization_barrier((after, before, columns))
            low, high = after[:2], before[2:]
            far_low = from_y(low, 1)
    copies = pl.pallas_call(
        last_row_kernel,
        out_shape=f32(ROW_PEERS, 2, 8, 128),
        in_specs=[SMEM, VMEM, VMEM, VMEM],
        out_specs=VMEM,
        scratch_shapes=row_scratch,
        compiler_params=params(8),
        name="last_row_sums",
    )(pos, columns, expd, total)
    sums = exchange(copies, ("z", "xh", "xl"))
    copies = pl.pallas_call(
        scales_kernel,
        out_shape=f32(2, 8, 128),
        in_specs=[VMEM],
        out_specs=VMEM,
        compiler_params=params(8),
        name="scales",
    )(sums)
    scales = [copies] + [from_y(copies, k) for k in range(1, 4)]
    row_blocks = [[own_rows], [after], [far_low, far_high], [before]]

    def grad_of(halves, blocks, sums_so_far, name):
        operands = [shelves[4 * half] for half in halves] + [scales[block] for block in blocks]
        operands += [piece for block in blocks for piece in row_blocks[block]] + sums_so_far
        return pl.pallas_call(
            functools.partial(grad_kernel, halves, blocks),
            out_shape=[f32(OWNED, D)] * len(halves),
            in_specs=[SMEM] + [VMEM] * (1 + len(operands)),
            out_specs=[VMEM] * len(halves),
            scratch_shapes=[pltpu.VMEM((OWNED, 128), jnp.float32)],
            compiler_params=params(8),
            cost_estimate=cost(3 * len(halves) * len(blocks) * HELD * OWNED, 6 * MIB),
            name=name,
        )(pos, columns, *operands)

    own, away = grad_of((0, 1), (0,), [], "grad_of_own_rows")
    (away,) = grad_of((1,), (1, 3, 2), [away], "grad_of_other")
    own, away = lax.optimization_barrier((own, away))
    other = from_core(away)
    (own,) = grad_of((0,), (1, 3, 2), [own], "grad_of_own")
    block = pl.BlockSpec((1, OWNED // 2, D), lambda i: (0, i, 0))
    return pl.pallas_call(
        update_kernel,
        out_shape=(f32(1, OWNED, D),) * 4,
        grid=(2,),
        in_specs=[pl.BlockSpec((OWNED // 2, D), lambda i: (i, 0))] * 2 + [block] * 3,
        out_specs=(block,) * 4,
        compiler_params=params(16),
        name="update",
    )(own, other, prototypes, moment_first, moment_second)


def solution(mesh):
    fine = Mesh(mesh.devices.reshape(2, 8, 2, 4, 2), ("xh", "z", "c", "y", "xl"))
    dp, proto = ("xh", "z", "c"), ("y", "xl")
    owned = P(proto, dp, None)
    return jax.shard_map(
        body,
        mesh=fine,
        in_specs=(P(dp, None), P(dp, None), owned, owned, owned),
        out_specs=(owned, owned, owned, owned),
        check_vma=False,
    )
```

```python
import functools
import math

import jax
import jax.numpy as jnp
from jax import lax
from jax.experimental import pallas as pl
from jax.experimental.pallas import tpu as pltpu
from jax.sharding import Mesh, PartitionSpec as P

K = 131072
ITERS = 3
D = 256
OWNED = 512
HELD = 1024
PART = 32
PLANES = 8
GROUP = 8
BATCH = 8192
ROW_PEERS = 32
LOG2E = math.log2(math.e)
FIRST_SCALE = LOG2E / 0.05
SECOND_SCALE = LOG2E / 0.1
GRAD_SCALE = K / (32 * 0.1)
MIB = 1 << 20

VMEM = pl.BlockSpec(memory_space=pltpu.VMEM)
HBM = pl.BlockSpec(memory_space=pltpu.HBM)
ANY = pl.BlockSpec(memory_space=pl.ANY)
SMEM = pl.BlockSpec(memory_space=pltpu.SMEM)


def normalize(values):
    values = values.astype(jnp.float32)
    return values / jnp.sqrt(jnp.sum(values * values, axis=-1, keepdims=True) + 1e-06)


def contract_last(left, right):
    return lax.dot_general(
        left, right, (((1,), (1,)), ((), ())), preferred_element_type=jnp.float32
    )


def place_of(pos_ref, block):
    return (pos_ref[0] + block // 4) % 2 * 4 + (pos_ref[1] + block % 4) % 4


def book_kernel(proto_ref, book_ref):
    book_ref[...] = normalize(proto_ref[0]).astype(jnp.bfloat16)


def views_kernel(views_ref, share_ref):
    for view in range(2):
        rows = normalize(views_ref[view]).astype(jnp.bfloat16)
        for peer in range(share_ref.shape[0]):
            share_ref[peer, view] = rows


def rows_of(rows_ref, view, at):
    return rows_ref[at // 256, :, view].reshape(256, D)


def copies_of_columns(pos_ref, columns, out_ref):
    line = lax.broadcasted_iota(jnp.int32, (GROUP, OWNED), 0)
    placed = jnp.zeros((GROUP, OWNED), jnp.float32)
    for block, values in enumerate(columns):
        placed = jnp.where(line == place_of(pos_ref, block), values, placed)
    for peer in range(GROUP):
        out_ref[peer] = placed


def expo_kernel(pos_ref, rows_ref, *refs):
    shelves, (expd_ref, out_ref) = refs[:GROUP], refs[GROUP:]
    columns = []
    for block in range(GROUP):
        shelf = shelves[block][...]
        total = jnp.zeros((8, OWNED), jnp.float32)
        for at in range(0, HELD, 256):
            tile = jnp.exp2(contract_last(rows_of(rows_ref, 0, at), shelf) * FIRST_SCALE)
            expd_ref[block, at : at + 256, :] = tile
            total = total + jnp.sum(tile.reshape(32, 8, OWNED), axis=0)
        columns.append(jnp.sum(total, axis=0, keepdims=True))
    copies_of_columns(pos_ref, columns, out_ref)


def rows_as_lanes(partial_ref):
    lines = [
        jnp.sum(partial_ref[j * 128 : (j + 1) * 128, :].T, axis=0, keepdims=True) for j in range(HELD // 128)
    ]
    return jnp.concatenate(lines, axis=0)


def row_kernel(pos_ref, columns_ref, expd_ref, out_ref, scale_ref, partial_ref):
    scale_a = 1.0 / (K * jnp.sum(columns_ref[...], axis=0))
    line = lax.broadcasted_iota(jnp.int32, (GROUP, OWNED), 0)
    for block in range(GROUP):
        picked = jnp.sum(jnp.where(line == place_of(pos_ref, block), scale_a, 0.0), axis=0, keepdims=True)
        scale_ref[block] = jnp.broadcast_to(picked, (8, OWNED))

    def step(i, carry):
        at = pl.ds(pl.multiple_of(i * 64, 64), 64)
        total = jnp.zeros((8, 8, 128), jnp.float32)
        for block in range(GROUP):
            for lane in range(0, OWNED, 128):
                tile = expd_ref[block, at, lane : lane + 128].reshape(8, 8, 128)
                total = total + tile * scale_ref[block, :, lane : lane + 128][None]
        partial_ref[at, :] = total.reshape(64, 128)
        return carry

    lax.fori_loop(0, HELD // 64, step, 0, unroll=16)
    lines = rows_as_lanes(partial_ref)
    for peer in range(ROW_PEERS):
        out_ref[peer] = lines


def last_row_kernel(pos_ref, columns_ref, expd_ref, total_ref, out_ref, scale_ref, partial_ref):
    row_kernel(pos_ref, columns_ref, expd_ref, out_ref.at[:, 0], scale_ref, partial_ref)
    for peer in range(ROW_PEERS):
        out_ref[peer, 1] = total_ref[...]


def column_kernel(pos_ref, sums_ref, expd_ref, out_ref, scale_ref):
    scale_b = 1.0 / (BATCH * jnp.sum(sums_ref[...], axis=0))
    for j in range(HELD // 128):
        scale_ref[j * 128 : (j + 1) * 128, :] = jnp.broadcast_to(scale_b[j : j + 1, :], (128, 128)).T

    def step(i, totals):
        at = pl.ds(pl.multiple_of(i * 8, 8), 8)
        scale = scale_ref[at, :]
        return tuple(
            totals[4 * block + j] + expd_ref[block, at, 128 * j : 128 * j + 128] * scale
            for block in range(GROUP)
            for j in range(4)
        )

    zero = jnp.zeros((8, 128), jnp.float32)
    totals = lax.fori_loop(0, HELD // 8, step, (zero,) * (4 * GROUP), unroll=16)
    columns = [
        jnp.sum(jnp.concatenate(totals[4 * block : 4 * block + 4], axis=1), axis=0, keepdims=True)
        for block in range(GROUP)
    ]
    copies_of_columns(pos_ref, columns, out_ref)


def total_kernel(rows_ref, *refs):
    shelves, (out_ref, partial_ref) = refs[:GROUP], refs[GROUP:]
    partial_ref[...] = jnp.zeros_like(partial_ref)
    for block in range(GROUP):
        shelf = shelves[block][...]
        for at in range(0, HELD, 256):
            tile = jnp.exp2(contract_last(rows_of(rows_ref, 1, at), shelf) * SECOND_SCALE)
            partial_ref[at : at + 256, :] += sum(tile[:, lane : lane + 128] for lane in range(0, OWNED, 128))
    out_ref[...] = rows_as_lanes(partial_ref)


def scales_kernel(sums_ref, out_ref):
    out_ref[...] = GRAD_SCALE / jnp.sum(sums_ref[...], axis=0)


def grad_kernel(halves, blocks, pos_ref, columns_ref, *refs):
    count = len(halves)
    refs = list(refs)
    books = [refs.pop(0) for _ in halves]
    scales = [refs.pop(0) for _ in blocks]
    rows = [[refs.pop(0) for _ in range(2 if block == 2 else 1)] for block in blocks]
    before = [refs.pop(0) for _ in halves] if 0 not in blocks else None
    outs, scale_ref = refs[:count], refs[count]
    scale_a = 1.0 / (K * jnp.sum(columns_ref[...], axis=0))
    line = lax.broadcasted_iota(jnp.int32, (GROUP, OWNED), 0)
    for i, half in enumerate(halves):
        picked = jnp.sum(jnp.where(line == place_of(pos_ref, 4 * half), scale_a, 0.0), axis=0, keepdims=True)
        for j in range(OWNED // 128):
            scale_ref[j * 128 : (j + 1) * 128, :] = jnp.broadcast_to(
                picked[:, j * 128 : (j + 1) * 128], (128, 128)
            ).T
        book = books[i][...]
        fresh = before is None
        for pieces, scale in zip(rows, scales):
            scale_b, scale_z = scale[0], scale[1]
            size = HELD // len(pieces)
            for at in range(0, HELD, 256):
                piece = pieces[at // size]
                two = rows_of(piece, 1, at % size)
                codes = jnp.exp2(contract_last(book, rows_of(piece, 0, at % size)) * FIRST_SCALE)
                probs = jnp.exp2(contract_last(book, two) * SECOND_SCALE)
                tiles = []
                for j in range(0, 256, 128):
                    row = (at + j) // 128
                    tiles.append(
                        (
                            probs[:, j : j + 128] * scale_z[row : row + 1, :]
                            - codes[:, j : j + 128] * scale_ref[...] * scale_b[row : row + 1, :]
                        ).astype(jnp.bfloat16)
                    )
                part = jnp.dot(jnp.concatenate(tiles, axis=1), two, preferred_element_type=jnp.float32)
                if fresh:
                    outs[i][...] = part
                elif before is not None and at == 0 and pieces is rows[0]:
                    outs[i][...] = before[i][...] + part
                else:
                    outs[i][...] += part
                fresh = False


def update_kernel(
    own_ref, other_ref, proto_ref, first_ref, second_ref, new_proto_ref, new_first_ref, new_second_ref, grad_ref
):
    grad = own_ref[...] + other_ref[...]
    new_first = 0.9 * first_ref[0] + 0.1 * grad
    new_second = 0.95 * second_ref[0] + 0.05 * grad * grad
    grad_ref[0] = grad
    new_first_ref[0] = new_first
    new_second_ref[0] = new_second
    new_proto_ref[0] = normalize(proto_ref[0]) - 0.05 * new_first / (jnp.sqrt(new_second) + 1e-08)


def params(mib):
    return pltpu.CompilerParams(vmem_limit_bytes=mib * MIB)


def f32(*shape):
    return jax.ShapeDtypeStruct(shape, jnp.float32)


def bf16(*shape):
    return jax.ShapeDtypeStruct(shape, jnp.bfloat16)


def cost(elements, size):
    return pl.CostEstimate(flops=2 * elements * D, bytes_accessed=size, transcendentals=elements)


def body(view_one, view_two, prototypes, moment_first, moment_second):
    pos = jnp.stack([lax.axis_index(name) for name in ("c", "y", "xl")]).astype(jnp.int32)

    def exchange(copies, axes):
        return lax.all_to_all(copies, axes, 0, 0, tiled=True)

    def from_y(values, distance):
        return lax.ppermute(values, "y", [((i + distance) % 4, i) for i in range(4)])

    def from_core(values):
        return lax.ppermute(values, "c", [(0, 1), (1, 0)])

    book = pl.pallas_call(
        book_kernel,
        out_shape=bf16(OWNED, D),
        in_specs=[VMEM],
        out_specs=VMEM,
        compiler_params=params(8),
        name="book",
    )(prototypes)
    start = (2 * pos[1] + pos[2]) * PART
    parts = jnp.stack([lax.dynamic_slice_in_dim(view, start, PART) for view in (view_one, view_two)])
    share = pl.pallas_call(
        views_kernel,
        out_shape=bf16(PLANES, 2, PART, D),
        in_specs=[VMEM],
        out_specs=VMEM,
        compiler_params=params(8),
        name="views",
    )(parts)
    shelves = [book] + [from_y(book, k) for k in range(1, 4)]
    share = exchange(share, ("z",))
    shelves[1], shelves[3], share = lax.optimization_barrier((shelves[1], shelves[3], share))
    shelves += [from_core(shelf) for shelf in shelves]
    own_rows = exchange(jnp.broadcast_to(share[None], (4,) + share.shape), ("xl", "xh"))

    expd, copies = pl.pallas_call(
        expo_kernel,
        out_shape=(f32(GROUP, HELD, OWNED), f32(GROUP, GROUP, OWNED)),
        in_specs=[SMEM] + [VMEM] * (1 + GROUP),
        out_specs=(VMEM, VMEM),
        compiler_params=params(8),
        name="expo",
    )(pos, own_rows, *shelves)
    columns = exchange(copies, ("c", "y"))
    sent, columns = lax.optimization_barrier((own_rows, columns))
    after, before = from_y(sent, 1), from_y(sent, -1)
    total = pl.pallas_call(
        total_kernel,
        out_shape=f32(8, 128),
        in_specs=[VMEM] * (1 + GROUP),
        out_specs=VMEM,
        scratch_shapes=[pltpu.VMEM((HELD, 128), jnp.float32)],
        compiler_params=params(8),
        cost_estimate=cost(HELD * GROUP * OWNED, 3 * MIB),
        name="totals",
    )(sent, *shelves)
    columns, total = lax.optimization_barrier((columns, total))
    row_scratch = [pltpu.VMEM((GROUP, 8, OWNED), jnp.float32), pltpu.VMEM((HELD, 128), jnp.float32)]
    assert ITERS == 3
    for step in range(ITERS - 1):
        copies = pl.pallas_call(
            row_kernel,
            out_shape=f32(ROW_PEERS, 8, 128),
            in_specs=[SMEM, VMEM, VMEM],
            out_specs=VMEM,
            scratch_shapes=row_scratch,
            compiler_params=params(8),
            name="row_sums",
        )(pos, columns, expd)
        if step == 1:
            high, copies = lax.optimization_barrier((high, copies))
            far_high = from_y(high, -1)
        sums = exchange(copies, ("z", "xh", "xl"))
        copies = pl.pallas_call(
            column_kernel,
            out_shape=f32(GROUP, GROUP, OWNED),
            in_specs=[SMEM, VMEM, VMEM],
            out_specs=VMEM,
            scratch_shapes=[pltpu.VMEM((HELD, 128), jnp.float32)],
            compiler_params=params(8),
            name="column_sums",
        )(pos, sums, expd)
        if step == 0:
            after, before, copies = lax.optimization_barrier((after, before, copies))
        else:
            far_low, far_high, copies = lax.optimization_barrier((far_low, far_high, copies))
        columns = exchange(copies, ("c", "y"))
        if step == 0:
            after, before, columns = lax.optimization_barrier((after, before, columns))
            low, high = after[:2], before[2:]
            far_low = from_y(low, 1)
    copies = pl.pallas_call(
        last_row_kernel,
        out_shape=f32(ROW_PEERS, 2, 8, 128),
        in_specs=[SMEM, VMEM, VMEM, VMEM],
        out_specs=VMEM,
        scratch_shapes=row_scratch,
        compiler_params=params(8),
        name="last_row_sums",
    )(pos, columns, expd, total)
    sums = exchange(copies, ("z", "xh", "xl"))
    copies = pl.pallas_call(
        scales_kernel,
        out_shape=f32(2, 8, 128),
        in_specs=[VMEM],
        out_specs=VMEM,
        compiler_params=params(8),
        name="scales",
    )(sums)
    scales = [copies] + [from_y(copies, k) for k in range(1, 4)]
    row_blocks = [[own_rows], [after], [far_low, far_high], [before]]

    def grad_of(halves, blocks, sums_so_far, name):
        operands = [shelves[4 * half] for half in halves] + [scales[block] for block in blocks]
        operands += [piece for block in blocks for piece in row_blocks[block]] + sums_so_far
        return pl.pallas_call(
            functools.partial(grad_kernel, halves, blocks),
            out_shape=[f32(OWNED, D)] * len(halves),
            in_specs=[SMEM] + [VMEM] * (1 + len(operands)),
            out_specs=[VMEM] * len(halves),
            scratch_shapes=[pltpu.VMEM((OWNED, 128), jnp.float32)],
            compiler_params=params(8),
            cost_estimate=cost(3 * len(halves) * len(blocks) * HELD * OWNED, 6 * MIB),
            name=name,
        )(pos, columns, *operands)

    own, away = grad_of((0, 1), (0,), [], "grad_of_own_rows")
    (away,) = grad_of((1,), (1, 3, 2), [away], "grad_of_other")
    own, away = lax.optimization_barrier((own, away))
    other = from_core(away)
    (own,) = grad_of((0,), (1, 3, 2), [own], "grad_of_own")
    block = pl.BlockSpec((1, OWNED // 2, D), lambda i: (0, i, 0))
    return pl.pallas_call(
        update_kernel,
        out_shape=(f32(1, OWNED, D),) * 4,
        grid=(2,),
        in_specs=[pl.BlockSpec((OWNED // 2, D), lambda i: (i, 0))] * 2 + [block] * 3,
        out_specs=(block,) * 4,
        compiler_params=params(16),
        name="update",
    )(own, other, prototypes, moment_first, moment_second)


def solution(mesh):
    fine = Mesh(mesh.devices.reshape(2, 8, 2, 4, 2), ("xh", "z", "c", "y", "xl"))
    dp, proto = ("xh", "z", "c"), ("y", "xl")
    owned = P(proto, dp, None)
    return jax.shard_map(
        body,
        mesh=fine,
        in_specs=(P(dp, None), P(dp, None), owned, owned, owned),
        out_specs=(owned, owned, owned, owned),
        check_vma=False,
    )
```

```python
import functools
import math

import jax
import jax.numpy as jnp
from jax import lax
from jax.experimental import pallas as pl
from jax.experimental.pallas import tpu as pltpu
from jax.sharding import Mesh, PartitionSpec as P

K = 131072
ITERS = 3
D = 256
OWNED = 512
HELD = 1024
PART = 32
PLANES = 8
GROUP = 8
BATCH = 8192
ROW_PEERS = 32
LOG2E = math.log2(math.e)
FIRST_SCALE = LOG2E / 0.05
SECOND_SCALE = LOG2E / 0.1
GRAD_SCALE = K / (32 * 0.1)
MIB = 1 << 20

VMEM = pl.BlockSpec(memory_space=pltpu.VMEM)
HBM = pl.BlockSpec(memory_space=pltpu.HBM)
ANY = pl.BlockSpec(memory_space=pl.ANY)
SMEM = pl.BlockSpec(memory_space=pltpu.SMEM)


def normalize(values):
    values = values.astype(jnp.float32)
    return values / jnp.sqrt(jnp.sum(values * values, axis=-1, keepdims=True) + 1e-06)


def contract_last(left, right):
    return lax.dot_general(
        left, right, (((1,), (1,)), ((), ())), preferred_element_type=jnp.float32
    )


def place_of(pos_ref, block):
    return (pos_ref[0] + block // 4) % 2 * 4 + (pos_ref[1] + block % 4) % 4


def book_kernel(proto_ref, book_ref):
    book_ref[...] = normalize(proto_ref[0]).astype(jnp.bfloat16)


def views_kernel(views_ref, share_ref):
    for view in range(2):
        rows = normalize(views_ref[view]).astype(jnp.bfloat16)
        for peer in range(share_ref.shape[0]):
            share_ref[peer, view] = rows


def rows_of(rows_ref, view, at):
    return rows_ref[at // 256, :, view].reshape(256, D)


def copies_of_columns(pos_ref, columns, out_ref):
    line = lax.broadcasted_iota(jnp.int32, (GROUP, OWNED), 0)
    placed = jnp.zeros((GROUP, OWNED), jnp.float32)
    for block, values in enumerate(columns):
        placed = jnp.where(line == place_of(pos_ref, block), values, placed)
    for peer in range(GROUP):
        out_ref[peer] = placed


def expo_kernel(pos_ref, rows_ref, *refs):
    shelves, (expd_ref, out_ref) = refs[:GROUP], refs[GROUP:]
    columns = []
    for block in range(GROUP):
        shelf = shelves[block][...]
        total = jnp.zeros((8, OWNED), jnp.float32)
        for at in range(0, HELD, 256):
            tile = jnp.exp2(contract_last(rows_of(rows_ref, 0, at), shelf) * FIRST_SCALE)
            expd_ref[block, at : at + 256, :] = tile
            total = total + jnp.sum(tile.reshape(32, 8, OWNED), axis=0)
        columns.append(jnp.sum(total, axis=0, keepdims=True))
    copies_of_columns(pos_ref, columns, out_ref)


def rows_as_lanes(partial_ref):
    lines = [
        jnp.sum(partial_ref[j * 128 : (j + 1) * 128, :].T, axis=0, keepdims=True) for j in range(HELD // 128)
    ]
    return jnp.concatenate(lines, axis=0)


def row_kernel(pos_ref, columns_ref, expd_ref, out_ref, scale_ref, partial_ref):
    scale_a = 1.0 / (K * jnp.sum(columns_ref[...], axis=0))
    line = lax.broadcasted_iota(jnp.int32, (GROUP, OWNED), 0)
    for block in range(GROUP):
        picked = jnp.sum(jnp.where(line == place_of(pos_ref, block), scale_a, 0.0), axis=0, keepdims=True)
        scale_ref[block] = jnp.broadcast_to(picked, (8, OWNED))

    def step(i, carry):
        at = pl.ds(pl.multiple_of(i * 64, 64), 64)
        total = jnp.zeros((8, 8, 128), jnp.float32)
        for block in range(GROUP):
            for lane in range(0, OWNED, 128):
                tile = expd_ref[block, at, lane : lane + 128].reshape(8, 8, 128)
                total = total + tile * scale_ref[block, :, lane : lane + 128][None]
        partial_ref[at, :] = total.reshape(64, 128)
        return carry

    lax.fori_loop(0, HELD // 64, step, 0, unroll=16)
    lines = rows_as_lanes(partial_ref)
    for peer in range(ROW_PEERS):
        out_ref[peer] = lines


def last_row_kernel(pos_ref, columns_ref, expd_ref, total_ref, out_ref, scale_ref, partial_ref):
    row_kernel(pos_ref, columns_ref, expd_ref, out_ref.at[:, 0], scale_ref, partial_ref)
    for peer in range(ROW_PEERS):
        out_ref[peer, 1] = total_ref[...]


def column_kernel(pos_ref, sums_ref, expd_ref, out_ref, scale_ref):
    scale_b = 1.0 / (BATCH * jnp.sum(sums_ref[...], axis=0))
    for j in range(HELD // 128):
        scale_ref[j * 128 : (j + 1) * 128, :] = jnp.broadcast_to(scale_b[j : j + 1, :], (128, 128)).T

    def step(i, totals):
        at = pl.ds(pl.multiple_of(i * 8, 8), 8)
        scale = scale_ref[at, :]
        return tuple(
            totals[4 * block + j] + expd_ref[block, at, 128 * j : 128 * j + 128] * scale
            for block in range(GROUP)
            for j in range(4)
        )

    zero = jnp.zeros((8, 128), jnp.float32)
    totals = lax.fori_loop(0, HELD // 8, step, (zero,) * (4 * GROUP), unroll=16)
    columns = [
        jnp.sum(jnp.concatenate(totals[4 * block : 4 * block + 4], axis=1), axis=0, keepdims=True)
        for block in range(GROUP)
    ]
    copies_of_columns(pos_ref, columns, out_ref)


def total_kernel(rows_ref, *refs):
    shelves, (out_ref, partial_ref) = refs[:GROUP], refs[GROUP:]
    partial_ref[...] = jnp.zeros_like(partial_ref)
    for block in range(GROUP):
        shelf = shelves[block][...]
        for at in range(0, HELD, 256):
            tile = jnp.exp2(contract_last(rows_of(rows_ref, 1, at), shelf) * SECOND_SCALE)
            partial_ref[at : at + 256, :] += sum(tile[:, lane : lane + 128] for lane in range(0, OWNED, 128))
    out_ref[...] = rows_as_lanes(partial_ref)


def scales_kernel(sums_ref, out_ref):
    out_ref[...] = GRAD_SCALE / jnp.sum(sums_ref[...], axis=0)


def grad_kernel(halves, blocks, pos_ref, columns_ref, *refs):
    count = len(halves)
    refs = list(refs)
    books = [refs.pop(0) for _ in halves]
    scales = [refs.pop(0) for _ in blocks]
    rows = [[refs.pop(0) for _ in range(2 if block == 2 else 1)] for block in blocks]
    before = [refs.pop(0) for _ in halves] if 0 not in blocks else None
    outs, weights = (refs[:count], refs[count:]) if before is None else (refs[count:], refs[:count])
    for i, half in enumerate(halves):
        scale_ref = weights[i]
        if before is None:
            scale_a = 1.0 / (K * jnp.sum(columns_ref[...], axis=0))
            line = lax.broadcasted_iota(jnp.int32, (GROUP, OWNED), 0)
            picked = jnp.sum(jnp.where(line == place_of(pos_ref, 4 * half), scale_a, 0.0), axis=0, keepdims=True)
            for j in range(OWNED // 128):
                scale_ref[j * 128 : (j + 1) * 128, :] = jnp.broadcast_to(
                    picked[:, j * 128 : (j + 1) * 128], (128, 128)
                ).T
        book = books[i][...]
        fresh = before is None
        for pieces, scale in zip(rows, scales):
            scale_b, scale_z = scale[0], scale[1]
            size = HELD // len(pieces)
            for at in range(0, HELD, 256):
                piece = pieces[at // size]
                two = rows_of(piece, 1, at % size)
                codes = jnp.exp2(contract_last(book, rows_of(piece, 0, at % size)) * FIRST_SCALE)
                probs = jnp.exp2(contract_last(book, two) * SECOND_SCALE)
                tiles = []
                for j in range(0, 256, 128):
                    row = (at + j) // 128
                    tiles.append(
                        (
                            probs[:, j : j + 128] * scale_z[row : row + 1, :]
                            - codes[:, j : j + 128] * scale_ref[...] * scale_b[row : row + 1, :]
                        ).astype(jnp.bfloat16)
                    )
                part = jnp.dot(jnp.concatenate(tiles, axis=1), two, preferred_element_type=jnp.float32)
                if fresh:
                    outs[i][...] = part
                elif before is not None and at == 0 and pieces is rows[0]:
                    outs[i][...] = before[i][...] + part
                else:
                    outs[i][...] += part
                fresh = False


def update_kernel(
    own_ref, other_ref, proto_ref, first_ref, second_ref, new_proto_ref, new_first_ref, new_second_ref, grad_ref
):
    grad = own_ref[...] + other_ref[...]
    new_first = 0.9 * first_ref[0] + 0.1 * grad
    new_second = 0.95 * second_ref[0] + 0.05 * grad * grad
    grad_ref[0] = grad
    new_first_ref[0] = new_first
    new_second_ref[0] = new_second
    new_proto_ref[0] = normalize(proto_ref[0]) - 0.05 * new_first / (jnp.sqrt(new_second) + 1e-08)


def params(mib):
    return pltpu.CompilerParams(vmem_limit_bytes=mib * MIB)


def f32(*shape):
    return jax.ShapeDtypeStruct(shape, jnp.float32)


def bf16(*shape):
    return jax.ShapeDtypeStruct(shape, jnp.bfloat16)


def cost(elements, size):
    return pl.CostEstimate(flops=2 * elements * D, bytes_accessed=size, transcendentals=elements)


def body(view_one, view_two, prototypes, moment_first, moment_second):
    pos = jnp.stack([lax.axis_index(name) for name in ("c", "y", "xl")]).astype(jnp.int32)

    def exchange(copies, axes):
        return lax.all_to_all(copies, axes, 0, 0, tiled=True)

    def from_y(values, distance):
        return lax.ppermute(values, "y", [((i + distance) % 4, i) for i in range(4)])

    def from_core(values):
        return lax.ppermute(values, "c", [(0, 1), (1, 0)])

    book = pl.pallas_call(
        book_kernel,
        out_shape=bf16(OWNED, D),
        in_specs=[VMEM],
        out_specs=VMEM,
        compiler_params=params(8),
        name="book",
    )(prototypes)
    start = (2 * pos[1] + pos[2]) * PART
    parts = jnp.stack([lax.dynamic_slice_in_dim(view, start, PART) for view in (view_one, view_two)])
    share = pl.pallas_call(
        views_kernel,
        out_shape=bf16(PLANES, 2, PART, D),
        in_specs=[VMEM],
        out_specs=VMEM,
        compiler_params=params(8),
        name="views",
    )(parts)
    shelves = [book] + [from_y(book, k) for k in range(1, 4)]
    share = exchange(share, ("z",))
    shelves[1], shelves[3], share = lax.optimization_barrier((shelves[1], shelves[3], share))
    shelves += [from_core(shelf) for shelf in shelves]
    own_rows = exchange(jnp.broadcast_to(share[None], (4,) + share.shape), ("xl", "xh"))

    expd, copies = pl.pallas_call(
        expo_kernel,
        out_shape=(f32(GROUP, HELD, OWNED), f32(GROUP, GROUP, OWNED)),
        in_specs=[SMEM] + [VMEM] * (1 + GROUP),
        out_specs=(VMEM, VMEM),
        compiler_params=params(8),
        name="expo",
    )(pos, own_rows, *shelves)
    columns = exchange(copies, ("c", "y"))
    sent, columns = lax.optimization_barrier((own_rows, columns))
    after, before = from_y(sent, 1), from_y(sent, -1)
    total = pl.pallas_call(
        total_kernel,
        out_shape=f32(8, 128),
        in_specs=[VMEM] * (1 + GROUP),
        out_specs=VMEM,
        scratch_shapes=[pltpu.VMEM((HELD, 128), jnp.float32)],
        compiler_params=params(8),
        cost_estimate=cost(HELD * GROUP * OWNED, 3 * MIB),
        name="totals",
    )(sent, *shelves)
    columns, total = lax.optimization_barrier((columns, total))
    row_scratch = [pltpu.VMEM((GROUP, 8, OWNED), jnp.float32), pltpu.VMEM((HELD, 128), jnp.float32)]
    assert ITERS == 3
    for step in range(ITERS - 1):
        copies = pl.pallas_call(
            row_kernel,
            out_shape=f32(ROW_PEERS, 8, 128),
            in_specs=[SMEM, VMEM, VMEM],
            out_specs=VMEM,
            scratch_shapes=row_scratch,
            compiler_params=params(8),
            name="row_sums",
        )(pos, columns, expd)
        if step == 1:
            high, copies = lax.optimization_barrier((high, copies))
            far_high = from_y(high, -1)
        sums = exchange(copies, ("z", "xh", "xl"))
        copies = pl.pallas_call(
            column_kernel,
            out_shape=f32(GROUP, GROUP, OWNED),
            in_specs=[SMEM, VMEM, VMEM],
            out_specs=VMEM,
            scratch_shapes=[pltpu.VMEM((HELD, 128), jnp.float32)],
            compiler_params=params(8),
            name="column_sums",
        )(pos, sums, expd)
        if step == 0:
            after, before, copies = lax.optimization_barrier((after, before, copies))
        else:
            far_low, far_high, copies = lax.optimization_barrier((far_low, far_high, copies))
        columns = exchange(copies, ("c", "y"))
        if step == 0:
            after, before, columns = lax.optimization_barrier((after, before, columns))
            low, high = after[:2], before[2:]
            far_low = from_y(low, 1)
    copies = pl.pallas_call(
        last_row_kernel,
        out_shape=f32(ROW_PEERS, 2, 8, 128),
        in_specs=[SMEM, VMEM, VMEM, VMEM],
        out_specs=VMEM,
        scratch_shapes=row_scratch,
        compiler_params=params(8),
        name="last_row_sums",
    )(pos, columns, expd, total)
    sums = exchange(copies, ("z", "xh", "xl"))
    copies = pl.pallas_call(
        scales_kernel,
        out_shape=f32(2, 8, 128),
        in_specs=[VMEM],
        out_specs=VMEM,
        compiler_params=params(8),
        name="scales",
    )(sums)
    scales = [copies] + [from_y(copies, k) for k in range(1, 4)]
    row_blocks = [[own_rows], [after], [far_low, far_high], [before]]

    def grad_of(halves, blocks, sums_so_far, name):
        operands = [shelves[4 * half] for half in halves] + [scales[block] for block in blocks]
        operands += [piece for block in blocks for piece in row_blocks[block]] + sums_so_far
        return pl.pallas_call(
            functools.partial(grad_kernel, halves, blocks),
            out_shape=[f32(OWNED, D)] * len(halves) + ([] if sums_so_far else [f32(OWNED, 128)] * len(halves)),
            in_specs=[SMEM] + [VMEM] * (1 + len(operands)),
            out_specs=[VMEM] * (len(halves) * (1 if sums_so_far else 2)),
            compiler_params=params(8),
            cost_estimate=cost(3 * len(halves) * len(blocks) * HELD * OWNED, 6 * MIB),
            name=name,
        )(pos, columns, *operands)

    own, away, own_weights, away_weights = grad_of((0, 1), (0,), [], "grad_of_own_rows")
    (away,) = grad_of((1,), (1, 3, 2), [away, away_weights], "grad_of_other")
    own, away = lax.optimization_barrier((own, away))
    other = from_core(away)
    (own,) = grad_of((0,), (1, 3, 2), [own, own_weights], "grad_of_own")
    block = pl.BlockSpec((1, OWNED // 2, D), lambda i: (0, i, 0))
    return pl.pallas_call(
        update_kernel,
        out_shape=(f32(1, OWNED, D),) * 4,
        grid=(2,),
        in_specs=[pl.BlockSpec((OWNED // 2, D), lambda i: (i, 0))] * 2 + [block] * 3,
        out_specs=(block,) * 4,
        compiler_params=params(16),
        name="update",
    )(own, other, prototypes, moment_first, moment_second)


def solution(mesh):
    fine = Mesh(mesh.devices.reshape(2, 8, 2, 4, 2), ("xh", "z", "c", "y", "xl"))
    dp, proto = ("xh", "z", "c"), ("y", "xl")
    owned = P(proto, dp, None)
    return jax.shard_map(
        body,
        mesh=fine,
        in_specs=(P(dp, None), P(dp, None), owned, owned, owned),
        out_specs=(owned, owned, owned, owned),
        check_vma=False,
    )
```
